256 devices in a mesh: blk: 64 (over z, x_hi, y), group: 4 (over x_lo, core).
Axes of the slice: x: 4 (x_hi: 2, x_lo: 2; x = x_hi * 2 + x_lo), y: 4, z: 8, core: 2. Of those that a mesh axis runs over, the one named last changes fastest.
Arguments:
- image_embeds: bfloat16 [4, 6144, 1152], P('group', 'blk')
- text_embeds: bfloat16 [4, 6144, 1152], P('group', 'blk'), may hold values from -0.1875 to 0.1875
- positives: int32 [4, 6144], P('group', 'blk'), may hold values from 0 to 6143, each once within a row
- partner: int32 [4], replicated, may hold values from 0 to 3, each once
- log_temp: float32 [1], replicated, may hold values from 1.6 to 2.4
- bias: float32 [1], replicated, may hold values from -4 to -2
Outputs:
- image_grads: float32 [4, 6144, 1152], P('group', 'blk')
- text_grads: float32 [4, 6144, 1152], P('group', 'blk')
- loss: float32 [1], replicated
The draws below stay inside these ranges and needn't reach their ends.
Inputs may be any that keep to these rules, and one draw needn't show every extreme that they name: Each group's positives name every text row of its partner group exactly once. `partner`: every group is named exactly once.
All inputs are finite; a program needn't handle non-finite values.
Results may differ from the reference program's by a relative error of at most 0.0015.
Values may be sent and summed in bfloat16 or wider, within the bound.
A program may use at most 64 MiB of HBM per device.

```python
import math
import jax
import jax.numpy as jnp

D = 1152
BLOCKS = 64
GROUPS = 4
GROUP_ROWS = 6144
IMAGES = 24576


def draw_image_embeds(key, part):
    key = jax.random.fold_in(key, 11)
    first, second = jax.random.split(key)
    place = (jnp.arange(GROUPS, dtype=jnp.float32)[:, None] * GROUP_ROWS + jnp.arange(GROUP_ROWS, dtype=jnp.float32)[None, :]) / IMAGES
    jitter = jax.random.uniform(second, (GROUPS, GROUP_ROWS), jnp.float32, 0.7, 1.4)
    top_scale = 10.0
    values = jax.random.normal(first, (GROUPS, GROUP_ROWS, D), jnp.float32)
    scale = jnp.exp(place * math.log(top_scale)) * jitter / math.sqrt(D)
    return (values * scale[:, :, None]).astype(jnp.bfloat16)


def level_of(own_key, shape, shards, smallest, top_value):
    level, own = 1.0, jax.random.fold_in(own_key, 6)
    for position, blocks in shards:
        heights = jnp.exp(jax.random.uniform(jax.random.fold_in(own, position), (blocks,), jnp.float32, smallest / len(shards), top_value / len(shards)))
        level = level * jnp.repeat(heights, shape[position] // blocks).reshape([-1 if axis == position else 1 for axis in range(len(shape))])
    return level


def normal_values(rng, dims, scale, limit, shards=(), kind=jnp.bfloat16):
    gain = level_of(rng, dims, shards, -0.22, 0.18) if shards else 1.0
    result = jax.random.normal(rng, dims, jnp.float32) * scale * gain
    return jnp.minimum(jnp.maximum(result, -limit), limit).astype(kind)


def setup_inputs(seed: int = 0) -> dict:
    arg_keys = jax.random.split(jax.random.key(seed), 7)
    return {
        "image_embeds": draw_image_embeds(jax.random.fold_in(arg_keys[6], 71), 0),
        "text_embeds": normal_values(arg_keys[1], (GROUPS, GROUP_ROWS, D), D ** -0.5, 0.1875, ((0, 4), (1, 64))),
        "positives": jax.vmap(lambda own: jax.random.permutation(own, GROUP_ROWS))(jax.random.split(arg_keys[2], GROUPS)).reshape((GROUPS, GROUP_ROWS)).astype(jnp.int32),
        "partner": jax.random.permutation(arg_keys[3], GROUPS).astype(jnp.int32),
        "log_temp": jnp.clip(jax.random.uniform(arg_keys[4], (1,), jnp.float32, 1.6, 2.4), 1.6, 2.4),
        "bias": jnp.clip(jax.random.uniform(arg_keys[5], (1,), jnp.float32, -4.0, -2.0), -4.0, -2.0),
    }


def pair_block(images, texts, hits, temper, offset):
    logits = temper * jnp.dot(images, texts.T, preferred_element_type=jnp.float32) + offset
    hit_values = hits.astype(jnp.float32)
    losses = jax.nn.softplus(logits) - hit_values * logits
    slopes = (jax.nn.sigmoid(logits) - hit_values).astype(jnp.bfloat16)
    return jnp.sum(losses), slopes


def reference(image_embeds, text_embeds, positives, partner, log_temp, bias):
    temper = jnp.exp(log_temp[0])
    offset = bias[0]
    columns = jnp.arange(GROUP_ROWS, dtype=jnp.int32)
    image_list = []
    text_grads = jnp.zeros((GROUPS, GROUP_ROWS, D), jnp.float32)
    total = jnp.zeros((), jnp.float32)
    for group in range(GROUPS):
        texts = text_embeds[partner[group]]
        hits = positives[group][:, None] == columns[None, :]
        part, slopes = pair_block(image_embeds[group], texts, hits, temper, offset)
        image_list.append(temper * jnp.dot(slopes, texts, preferred_element_type=jnp.float32))
        back = temper * jnp.dot(slopes.T, image_embeds[group], preferred_element_type=jnp.float32)
        text_grads = text_grads.at[partner[group]].set(back)
        total = total + part
    loss = total / (IMAGES * BLOCKS)
    return jnp.stack(image_list), text_grads, jnp.reshape(loss, (1,))
```

```python
import jax
import jax.numpy as jnp
from jax import lax
from jax.sharding import PartitionSpec as P

LINE = 8


def pair_block(images, texts, hits, temper, offset):
    logits = temper * jnp.dot(images, texts.T, preferred_element_type=jnp.float32) + offset
    hit_values = hits.astype(jnp.float32)
    losses = jax.nn.softplus(logits) - hit_values * logits
    slopes = (jax.nn.sigmoid(logits) - hit_values).astype(jnp.bfloat16)
    return (jnp.sum(losses), slopes)


def shards(image_embeds, text_embeds, positives, partner, log_temp, bias):
    temper = jnp.exp(log_temp[0])
    offset = bias[0]
    images = image_embeds[0]
    own_texts = text_embeds[0]
    own_labels = positives[0]
    rows = images.shape[0]
    width = images.shape[1]
    cycle_size = lax.axis_size("blk")
    group_count = lax.axis_size("group")
    blk_place = lax.axis_index("blk")
    group_place = lax.axis_index("group")
    down = cycle_size // LINE
    across_groups = [[a * LINE + b for b in range(LINE)] for a in range(down)]
    down_groups = [[a * LINE + b for a in range(down)] for b in range(LINE)]

    every_text = lax.all_gather(own_texts, "group", axis=0, tiled=True)
    target = partner[group_place]
    partner_block = lax.dynamic_slice_in_dim(every_text, target * rows, rows, 0)

    tile_images = lax.all_gather(images, "blk", axis=0, tiled=True, axis_index_groups=across_groups)
    tile_labels = lax.all_gather(own_labels, "blk", axis=0, tiled=True, axis_index_groups=across_groups)
    tile_texts = lax.all_gather(partner_block, "blk", axis=0, tiled=True, axis_index_groups=down_groups)
    column = jnp.arange(down * rows, dtype=jnp.int32)
    owner = (column // rows) * LINE + blk_place % LINE
    column = owner * rows + column % rows
    hits = tile_labels[:, None] == column[None, :]
    part, slopes = pair_block(tile_images, tile_texts, hits, temper, offset)
    image_part = temper * jnp.dot(slopes, tile_texts, preferred_element_type=jnp.float32)
    text_part = temper * jnp.dot(slopes.T, tile_images, preferred_element_type=jnp.float32)
    image_sum = lax.psum_scatter(image_part, "blk", scatter_dimension=0, tiled=True, axis_index_groups=across_groups)
    text_sum = lax.psum_scatter(text_part, "blk", scatter_dimension=0, tiled=True, axis_index_groups=down_groups)

    every_grad = lax.all_gather(text_sum, "group", axis=0, tiled=True)
    source = jnp.argmax((partner == group_place).astype(jnp.int32))
    text_home = lax.dynamic_slice_in_dim(every_grad, source * rows, rows, 0)
    total = lax.psum(part, ("blk", "group"))
    loss = total / (group_count * rows * cycle_size * cycle_size)
    return (image_sum[None], text_home[None], jnp.reshape(loss, (1,)))


def solution(mesh):
    in_specs = (P("group", "blk", None), P("group", "blk", None), P("group", "blk"), P(), P(), P())
    out_specs = (P("group", "blk", None), P("group", "blk", None), P())
    return jax.shard_map(shards, mesh=mesh, in_specs=in_specs, out_specs=out_specs, check_vma=False)
```

```python
import functools

import jax
import jax.numpy as jnp
from jax import lax
from jax.experimental import pallas as pl
from jax.experimental.pallas import tpu as pltpu
from jax.sharding import PartitionSpec as P

NZ, NX, NY = 8, 4, 4
LANES = 128
SCALE_ROWS = 16
TOP = 14.9657842846620869


def kernel(total_pairs, partner_ref, temp_ref, bias_ref, img_ref, txt_ref, lab_in_ref,
           img_out, txt_out, loss_out,
           ibuf, tbuf, xbuf, labrow, labcol, slopes, slopes_t, gi, gt, tsum, loss_acc, loss_in,
           zq_out, zq_in, yq_out, yq_in, sq_out, sq_in, xq_out, xq_in,
           send_sems, recv_sems):
    rows, width = img_ref.shape[1], img_ref.shape[2]
    half = rows // 2
    tiles = width // LANES
    blk, group = lax.axis_index("blk"), lax.axis_index("group")
    z, x_hi, y = blk // (NX // 2 * NY), (blk // NY) % (NX // 2), blk % NY
    x_lo, core = group // 2, group % 2
    x = x_hi * 2 + x_lo

    def device(z_at, x_at, y_at, core_at):
        return (z_at * (NX // 2 * NY) + (x_at // 2) * NY + y_at, (x_at % 2) * 2 + core_at)

    def flipped(value, bit):
        return value + bit - 2 * bit * ((value // bit) % 2)

    z_up, z_down = device((z + 1) % NZ, x, y, core), device((z + NZ - 1) % NZ, x, y, core)
    y_up, y_down = device(z, x, (y + 1) % NY, core), device(z, x, (y + NY - 1) % NY, core)
    x_up, x_down = device(z, (x + 1) % NX, y, core), device(z, (x + NX - 1) % NX, y, core)
    twin = device(z, x, y, 1 - core)
    loss_peers = [twin, device(flipped(z, 1), x, y, core), device(flipped(z, 2), x, y, core),
                  device(flipped(z, 4), x, y, core), device(z, flipped(x, 1), y, core),
                  device(z, flipped(x, 2), y, core), device(z, x, flipped(y, 1), core),
                  device(z, x, flipped(y, 2), core)]

    greeted = [z_up, z_down, y_up, y_down, x_up, x_down, twin,
               loss_peers[2], loss_peers[3], loss_peers[5], loss_peers[7]]
    barrier = pltpu.get_barrier_semaphore()
    for peer in greeted:
        pl.semaphore_signal(barrier, inc=1, device_id=peer, device_id_type=pl.DeviceIdType.MESH)
    pl.semaphore_wait(barrier, len(greeted))

    places, pending = {}, []

    def copy_of(name, src, dst, peer):
        place = places.setdefault(name, len(places))
        return pltpu.make_async_remote_copy(
            src_ref=src, dst_ref=dst, send_sem=send_sems.at[place], recv_sem=recv_sems.at[place],
            device_id=peer, device_id_type=pl.DeviceIdType.MESH)

    def send(name, src, dst, peer):
        copy = copy_of(name, src, dst, peer)
        copy.start()
        pending.append(copy)

    def arrived(name, dst, peer):
        copy_of(name, dst, dst, peer).wait_recv()

    A, B = 0, 1

    def part(chunk):
        return pl.ds(chunk * half, half)

    def image_slot(rel, chunk):
        return ibuf.at[pl.ds((rel % NZ) * rows + chunk * half, half)]

    def text_slot(rel, p, chunk):
        return tbuf.at[pl.ds(((rel % NY) * 2 + p) * rows + chunk * half, half)]

    def x_slot(side, rel, chunk):
        return xbuf.at[side, rel % NX, part(chunk)]

    labrow[0] = jnp.zeros((8, LANES), jnp.int32)
    labrow[0, 0:1, 0:rows] = lab_in_ref[...]

    def z_send(hop, way, chunk):
        src = img_ref.at[0, part(chunk)] if hop == 1 else image_slot(-way * (hop - 1), chunk)
        send(("z", hop, way, chunk), src, image_slot(-way * hop, chunk), z_up if way > 0 else z_down)
        if chunk == (A if way > 0 else B) and (way > 0 or hop < NZ // 2):
            send(("label", hop, way), labrow.at[(-way * (hop - 1)) % NZ], labrow.at[(-way * hop) % NZ],
                 z_up if way > 0 else z_down)

    def z_arrived(hop, way, chunk):
        arrived(("z", hop, way, chunk), image_slot(-way * hop, chunk), z_up)
        if chunk == (A if way > 0 else B) and (way > 0 or hop < NZ // 2):
            arrived(("label", hop, way), labrow.at[(-way * hop) % NZ], z_up)

    def x_send(hop, way, chunk):
        src = txt_ref.at[0, part(chunk)] if hop == 1 else x_slot(0, -way * (hop - 1), chunk)
        send(("x", hop, way, chunk), src, x_slot(0, -way * hop, chunk), x_up if way > 0 else x_down)

    def x_arrived(hop, way, chunk):
        arrived(("x", hop, way, chunk), x_slot(0, -way * hop, chunk), x_up)

    def twin_send(rel, chunk):
        src = txt_ref.at[0, part(chunk)] if rel == 0 else x_slot(0, rel, chunk)
        send(("twin", rel, chunk), src, x_slot(1, rel, chunk), twin)

    def twin_arrived(rel, chunk):
        arrived(("twin", rel, chunk), x_slot(1, rel, chunk), twin)

    def y_send(hop, way, p, chunk):
        send(("y", hop, way, p, chunk), text_slot(-way * (hop - 1), p, chunk), text_slot(-way * hop, p, chunk),
             y_up if way > 0 else y_down)

    def y_arrived(hop, way, p, chunk):
        arrived(("y", hop, way, p, chunk), text_slot(-way * hop, p, chunk), y_up)

    target = partner_ref[group]
    same_side = target // 2 == x_lo
    same_core = target % 2 == core
    near = 1 + 2 * x_lo
    far = 3 - 2 * x_lo

    def choose(p, chunk):
        middle = [txt_ref[0, part(chunk)] if p == 0 else xbuf[0, 2, part(chunk)], xbuf[1, 2 * p, part(chunk)]]
        side_at = near if p == 0 else far
        side = [xbuf[0, side_at, part(chunk)], xbuf[1, side_at, part(chunk)]]
        middle = jnp.where(same_core, middle[0], middle[1])
        side = jnp.where(same_core, side[0], side[1])
        tbuf[pl.ds(p * rows + chunk * half, half), :] = jnp.where(same_side, middle, side)

    z_send(1, 1, A)
    x_send(1, 1, A)
    z_send(1, -1, B)
    x_send(1, -1, B)
    twin_send(0, A)
    twin_send(0, B)
    z_send(1, 1, B)
    z_send(1, -1, A)
    x_send(1, 1, B)
    x_send(1, -1, A)
    ibuf[0:rows, :] = img_ref[0]

    x_arrived(1, 1, A)
    x_send(2, 1, A)
    twin_send(3, A)
    x_arrived(1, -1, B)
    x_send(2, -1, B)
    twin_send(1, B)
    z_arrived(1, 1, A)
    z_send(2, 1, A)
    z_arrived(1, -1, B)
    z_send(2, -1, B)
    x_arrived(1, 1, B)
    twin_send(3, B)
    x_arrived(1, -1, A)
    twin_send(1, A)
    z_arrived(1, 1, B)
    z_send(2, 1, B)
    z_arrived(1, -1, A)
    z_send(2, -1, A)
    for chunk in (A, B):
        for rel in (0, 1, 3):
            twin_arrived(rel, chunk)
        choose(0, chunk)
        y_send(1, 1, 0, chunk)
        y_send(1, -1, 0, chunk)
    x_arrived(2, 1, A)
    twin_send(2, A)
    x_arrived(2, -1, B)
    twin_send(2, B)
    for chunk in (A, B):
        twin_arrived(2, chunk)
        choose(1, chunk)
        y_send(1, 1, 1, chunk)
        y_send(1, -1, 1, chunk)
    z_arrived(2, 1, A)
    z_send(3, 1, A)
    z_arrived(2, -1, B)
    z_send(3, -1, B)
    y_arrived(1, 1, 0, A)
    y_send(2, 1, 0, A)
    z_arrived(2, 1, B)
    z_send(3, 1, B)
    z_arrived(2, -1, A)
    z_send(3, -1, A)
    y_arrived(1, -1, 0, A)
    y_arrived(1, -1, 0, B)
    y_send(2, -1, 0, B)
    y_arrived(1, 1, 0, B)
    z_arrived(3, 1, A)
    z_send(4, 1, A)
    z_arrived(3, -1, B)
    z_send(4, -1, B)
    y_arrived(1, 1, 1, A)
    y_send(2, 1, 1, A)
    y_arrived(1, -1, 1, A)
    y_arrived(1, -1, 1, B)
    y_send(2, -1, 1, B)
    y_arrived(1, 1, 1, B)
    z_arrived(3, 1, B)
    z_arrived(3, -1, A)
    z_arrived(4, 1, A)
    z_arrived(4, -1, B)
    for p in (0, 1):
        y_arrived(2, 1, p, A)
        y_arrived(2, -1, p, B)

    temper = jnp.exp(jnp.full((1, LANES), temp_ref[0], jnp.float32))
    offset = jnp.full((1, LANES), bias_ref[0], jnp.float32)
    for rel in range(NZ):
        column = jnp.broadcast_to(labrow[rel, 0:1, :], (LANES, LANES)).T
        labcol[rel * rows:(rel + 1) * rows, :] = column[:rows]
    n_i, n_t = NZ * rows, 2 * NY * rows
    wide = 2 * LANES
    loss_acc[0] = jnp.zeros((8, LANES), jnp.float32)

    def slope_tile(step, carry):
        top = pl.multiple_of(step * wide, wide)
        images = ibuf[pl.ds(top, wide), :]
        for left in range(0, n_t, wide):
            dots = lax.dot_general(images, tbuf[left:left + wide, :], (((1,), (1,)), ((), ())),
                                   preferred_element_type=jnp.float32)
            for at in range(0, wide, LANES):
                logits = temper * dots[:, at:at + LANES] + offset
                column = lax.broadcasted_iota(jnp.int32, (1, LANES), 1) + (left + at)
                own = column + ((z * (NX // 2) + x_hi) * NY + y) * rows
                for b in range(1, 2 * NY):
                    owner = (z * (NX // 2) + (x_hi + b % 2) % 2) * NY + (y + b // 2) % NY
                    own = jnp.where(column >= b * rows, column + (owner - b) * rows, own)
                hit = labcol[pl.ds(top, wide), :] == own
                margin = jnp.where(hit, -logits, logits)
                small = jnp.exp(-jnp.abs(logits))
                base = 1.0 + small
                inverse = 1.0 / base
                log_part = jnp.log(base) + (small - (base - 1.0)) * inverse
                loss = jnp.maximum(margin, 0.0) + log_part
                loss_acc[0] += jnp.sum(loss.reshape(wide // 8, 8, LANES), axis=0)
                slope = jnp.where(margin >= 0.0, 1.0, small) * inverse
                slope = jnp.where(hit, -slope, slope).astype(jnp.bfloat16)
                slopes[pl.ds(top, wide), left + at:left + at + LANES] = slope
                slopes_t[left + at:left + at + LANES, pl.ds(top, wide)] = slope.T
        return carry

    lax.fori_loop(0, n_i // wide, slope_tile, 0)

    def grad_images(first, count):
        gi[first * rows:(first + count) * rows, :] = jnp.dot(
            slopes[first * rows:(first + count) * rows, :], tbuf[...], preferred_element_type=jnp.float32)

    def grad_texts(first, count):
        gt[first * rows:(first + count) * rows, :] = jnp.dot(
            slopes_t[first * rows:(first + count) * rows, :], ibuf[...], preferred_element_type=jnp.float32)

    def packed(out, value):
        tops = jnp.max(jnp.abs(value).reshape(half // SCALE_ROWS, SCALE_ROWS, width), axis=0)
        top = tops[:, 0:LANES]
        for t in range(1, tiles):
            top = jnp.maximum(top, tops[:, t * LANES:(t + 1) * LANES])
        exponent = jnp.ceil(jnp.log2(jnp.maximum(top, 1e-30)))
        inverse = jnp.concatenate([jnp.exp2(TOP - exponent)] * (half // SCALE_ROWS), axis=0)
        out[tiles * half:tiles * half + SCALE_ROWS, :] = exponent.astype(jnp.int16)
        for t in range(tiles):
            scaled = jnp.round(value[:, t * LANES:(t + 1) * LANES] * inverse)
            out[t * half:(t + 1) * half, :] = scaled.astype(jnp.int32).astype(jnp.int16)

    def unpacked(message):
        exponent = message[tiles * half:tiles * half + SCALE_ROWS, :].astype(jnp.int32).astype(jnp.float32)
        scale = jnp.concatenate([jnp.exp2(exponent - TOP)] * (half // SCALE_ROWS), axis=0)
        return jnp.concatenate(
            [message[t * half:(t + 1) * half, :].astype(jnp.int32).astype(jnp.float32) * scale for t in range(tiles)],
            axis=1)

    def ring(kind, n, out, inbox, up, down, partial):
        halfway = n // 2

        def slot(hop, way, chunk):
            return (0 if way > 0 else 1), 2 * (hop - 1) + chunk

        def get(hop, way, chunk):
            box = inbox.at[slot(hop, way, chunk)]
            arrived((kind, hop, way, chunk), box, up)
            return unpacked(box)

        def put(hop, way, chunk):
            value = partial(way * (halfway + 1 - hop), chunk)
            fresh = hop == 1 or (hop == 2 and chunk == (B if way > 0 else A))
            if not fresh:
                value = value + get(hop - 1, way, chunk)
            at = slot(hop, way, chunk)
            packed(out.at[at], value)
            send((kind, hop, way, chunk), out.at[at], inbox.at[at], up if way > 0 else down)

        def last(chunk):
            return partial(0, chunk) + get(halfway, 1, chunk) + get(halfway, -1, chunk)

        return put, last

    z_put, z_last = ring(
        "gz", NZ, zq_out, zq_in, z_up, z_down,
        lambda rel, chunk: gi[(rel % NZ) * rows + chunk * half:(rel % NZ) * rows + (chunk + 1) * half, :])
    y_puts, y_lasts = [], []
    for p in (0, 1):
        put, last = ring(
            ("gy", p), NY, yq_out.at[p], yq_in.at[p], y_up, y_down,
            lambda rel, chunk, p=p: gt[((rel % NY) * 2 + p) * rows + chunk * half:
                                       ((rel % NY) * 2 + p) * rows + (chunk + 1) * half, :])
        y_puts.append(put)
        y_lasts.append(last)

    def loss_step(step):
        send(("loss", step), loss_acc.at[step], loss_in.at[step], loss_peers[step])
        arrived(("loss", step), loss_in.at[step], twin)
        loss_acc[step + 1] = loss_acc[step] + loss_in[step]

    grad_images(3, 3)
    z_put(1, 1, A)
    z_put(1, -1, B)
    grad_texts(4, 2)
    y_puts[1](1, 1, A)
    y_puts[1](1, -1, B)
    z_put(2, 1, B)
    z_put(2, -1, A)
    y_puts[0](1, 1, A)
    y_puts[0](1, -1, B)
    grad_texts(2, 2)
    grad_texts(6, 2)
    y_puts[1](2, 1, B)
    y_puts[1](2, -1, A)
    z_put(2, 1, A)
    z_put(2, -1, B)
    y_puts[0](2, 1, B)
    y_puts[0](2, -1, A)
    y_puts[1](2, 1, A)
    y_puts[1](2, -1, B)
    grad_images(0, 3)
    grad_images(6, 2)
    grad_texts(0, 2)
    z_put(3, 1, B)
    z_put(3, -1, A)
    loss_step(0)
    y_puts[0](2, 1, A)
    y_puts[0](2, -1, B)
    z_put(3, 1, A)
    z_put(3, -1, B)
    loss_step(1)

    def twin_grad_send(p, chunk):
        packed(sq_out.at[p, chunk], tsum[p, part(chunk)])
        send(("gs", p, chunk), sq_out.at[p, chunk], sq_in.at[p, chunk], twin)

    def y_finish(p, chunk):
        tsum[p, part(chunk)] = y_lasts[p](chunk)
        twin_grad_send(p, chunk)

    twin_group = x_lo * 2 + (1 - core)
    twin_target = partner_ref[twin_group]
    across = (1 - x_lo) * 2 + core

    def weight(who, home):
        return jnp.full((1, LANES), jnp.where(who == home, 1.0, 0.0), jnp.float32)

    weights = {0: (weight(target, group), weight(twin_target, group)),
               1: (weight(target, across), weight(twin_target, across))}

    def x_partial(rel, chunk):
        rel = rel % NX
        p = {0: 0, 2: 1, 1: x_lo, 3: 1 - x_lo}[rel]
        own_weight, twin_weight = weights[rel % 2]
        own, other = tsum[p, part(chunk)], unpacked(sq_in.at[p, chunk])
        return jnp.concatenate(
            [own[:, t * LANES:(t + 1) * LANES] * own_weight + other[:, t * LANES:(t + 1) * LANES] * twin_weight
             for t in range(tiles)], axis=1)

    x_put, x_last = ring("gx", NX, xq_out, xq_in, x_up, x_down, x_partial)

    y_finish(1, A)
    y_finish(1, B)
    z_put(4, 1, B)
    z_put(4, -1, A)
    loss_step(2)
    for chunk in (A, B):
        arrived(("gs", 1, chunk), sq_in.at[1, chunk], twin)
    x_put(1, 1, A)
    x_put(1, -1, B)
    loss_step(3)
    y_finish(0, A)
    y_finish(0, B)
    z_put(4, 1, A)
    z_put(4, -1, B)
    loss_step(4)
    for chunk in (A, B):
        arrived(("gs", 0, chunk), sq_in.at[0, chunk], twin)
    x_put(2, 1, B)
    x_put(2, -1, A)
    loss_step(5)
    x_put(2, 1, A)
    x_put(2, -1, B)
    loss_step(6)
    loss_step(7)
    loss_out[0] = jnp.sum(loss_acc[8]) / total_pairs

    def write(out, chunk, value):
        for t in range(tiles):
            out[0, part(chunk), t * LANES:(t + 1) * LANES] = temper * value[:, t * LANES:(t + 1) * LANES]

    for chunk in (A, B):
        write(img_out, chunk, z_last(chunk))
    for chunk in (A, B):
        write(txt_out, chunk, x_last(chunk))
    for copy in pending:
        copy.wait_send()


def shards(image_embeds, text_embeds, positives, partner, log_temp, bias):
    _, rows, width = image_embeds.shape
    half, tiles = rows // 2, width // LANES
    message = (tiles * half + SCALE_ROWS, LANES)
    n_i, n_t = NZ * rows, 2 * NY * rows
    cycle, groups = lax.axis_size("blk"), lax.axis_size("group")
    total_pairs = groups * rows * cycle * cycle
    vmem = pl.BlockSpec(memory_space=pltpu.VMEM)
    smem = pl.BlockSpec(memory_space=pltpu.SMEM)
    f32, bf16, i16, i32 = jnp.float32, jnp.bfloat16, jnp.int16, jnp.int32
    copies = 160
    return pl.pallas_call(
        functools.partial(kernel, float(total_pairs)),
        out_shape=(jax.ShapeDtypeStruct((1, rows, width), f32), jax.ShapeDtypeStruct((1, rows, width), f32),
                   jax.ShapeDtypeStruct((1,), f32)),
        in_specs=[smem, smem, smem, vmem, vmem, vmem],
        out_specs=(vmem, vmem, smem),
        scratch_shapes=[
            pltpu.VMEM((n_i, width), bf16),
            pltpu.VMEM((n_t, width), bf16),
            pltpu.VMEM((2, NX, rows, width), bf16),
            pltpu.VMEM((NZ, 8, LANES), i32),
            pltpu.VMEM((n_i, LANES), i32),
            pltpu.VMEM((n_i, n_t), bf16),
            pltpu.VMEM((n_t, n_i), bf16),
            pltpu.VMEM((n_i, width), f32),
            pltpu.VMEM((n_t, width), f32),
            pltpu.VMEM((2, rows, width), f32),
            pltpu.VMEM((9, 8, LANES), f32),
            pltpu.VMEM((8, 8, LANES), f32),
            pltpu.VMEM((2, NZ, *message), i16),
            pltpu.VMEM((2, NZ, *message), i16),
            pltpu.VMEM((2, 2, NY, *message), i16),
            pltpu.VMEM((2, 2, NY, *message), i16),
            pltpu.VMEM((2, 2, *message), i16),
            pltpu.VMEM((2, 2, *message), i16),
            pltpu.VMEM((2, NX, *message), i16),
            pltpu.VMEM((2, NX, *message), i16),
            pltpu.SemaphoreType.DMA((copies,)),
            pltpu.SemaphoreType.DMA((copies,)),
        ],
        compiler_params=pltpu.CompilerParams(
            collective_id=0, has_side_effects=True, vmem_limit_bytes=48 * 1024 * 1024),
    )(partner, log_temp, bias, image_embeds, text_embeds, positives)


def solution(mesh):
    in_specs = (P("group", "blk", None), P("group", "blk", None), P("group", "blk"), P(), P(), P())
    out_specs = (P("group", "blk", None), P("group", "blk", None), P())
    return jax.shard_map(shards, mesh=mesh, in_specs=in_specs, out_specs=out_specs, check_vma=False)
```

```python
import functools

import jax
import jax.numpy as jnp
from jax import lax
from jax.experimental import pallas as pl
from jax.experimental.pallas import tpu as pltpu
from jax.sharding import PartitionSpec as P

NZ, NX, NY = 8, 4, 4
LANES = 128
SCALE_ROWS = 16
TOP = 14.9657842846620869


def kernel(total_pairs, partner_in, temp_in, bias_in, img_in, txt_in, lab_in,
           img_out, txt_out, loss_out,
           partner_ref, temp_ref, bias_ref, lab_own, ibuf, tbuf, xbuf, labrow, labcol, slopes, slopes_t, gi, gt, tsum,
           loss_acc, loss_in, zq_out, zq_in, yq_out, yq_in, sq_out, sq_in, xq_out, xq_in,
           send_sems, recv_sems, local_sems):
    rows, width = img_in.shape[1], img_in.shape[2]
    half = rows // 2
    tiles = width // LANES
    A, B = 0, 1
    OWN, NEAR, FAR, OPPOSITE = 0, 1, 2, 3

    local = [pltpu.make_async_copy(src, dst, local_sems.at[k]) for k, (src, dst) in enumerate((
        (txt_in.at[0], xbuf.at[0, OWN]), (img_in.at[0], ibuf.at[0:rows]), (lab_in, lab_own),
        (partner_in, partner_ref), (temp_in, temp_ref), (bias_in, bias_ref)))]
    for copy in local:
        copy.start()

    blk, group = lax.axis_index("blk"), lax.axis_index("group")
    z, x_hi, y = blk // (NX // 2 * NY), (blk // NY) % (NX // 2), blk % NY
    x_lo, core = group // 2, group % 2
    x = x_hi * 2 + x_lo

    def device(z_at, x_at, y_at, core_at):
        return ((z_at % NZ) * (NX // 2 * NY) + ((x_at % NX) // 2) * NY + y_at % NY, (x_at % 2) * 2 + core_at)

    z_up, z_down = device(z + 1, x, y, core), device(z + NZ - 1, x, y, core)
    y_up, y_down = device(z, x, y + 1, core), device(z, x, y + NY - 1, core)
    near, far = device(z, x + 1 + 2 * x_lo, y, core), device(z, x + 3 - 2 * x_lo, y, core)
    twin = device(z, x, y, 1 - core)
    x_others = [(d, device(z, x + d, y, core)) for d in range(1, NX)]
    y_others = [(d, device(z, x, y + d, core)) for d in range(1, NY)]
    z_others = [(d, device(z + d, x, y, core)) for d in range(1, NZ)]

    greeted = [twin] + [peer for _, peer in x_others + y_others + z_others]
    barrier = pltpu.get_barrier_semaphore()
    for peer in greeted:
        pl.semaphore_signal(barrier, inc=1, device_id=peer, device_id_type=pl.DeviceIdType.MESH)
    pl.semaphore_wait(barrier, len(greeted))

    places, pending = {}, []

    def copy_of(name, src, dst, peer):
        place = places.setdefault(name, len(places))
        return pltpu.make_async_remote_copy(
            src_ref=src, dst_ref=dst, send_sem=send_sems.at[place], recv_sem=recv_sems.at[place],
            device_id=peer, device_id_type=pl.DeviceIdType.MESH)

    def send(name, src, dst, peer):
        copy = copy_of(name, src, dst, peer)
        copy.start()
        pending.append(copy)

    def arrived(name, dst, peer):
        copy_of(name, dst, dst, peer).wait_recv()

    def part(chunk):
        return pl.ds(chunk * half, half)

    order = (0, 1, 7, 2, 6, 3, 5, 4)

    def image_at(rel, chunk=0):
        return order.index(rel % NZ) * rows + chunk * half

    def text_at(rel, p, chunk=0):
        return (p * NY + rel % NY) * rows + chunk * half

    def image_slot(rel, chunk):
        return ibuf.at[pl.ds(image_at(rel, chunk), half)]

    def text_slot(rel, p, chunk):
        return tbuf.at[pl.ds(text_at(rel, p, chunk), half)]

    def x_slot(side, which, chunk):
        return xbuf.at[side, which, part(chunk)]

    def z_send(hop, way, chunk):
        send(("z", hop, way, chunk), image_slot(-way * (hop - 1), chunk), image_slot(-way * hop, chunk),
             z_up if way > 0 else z_down)
        if chunk == (A if way > 0 else B) and (way > 0 or hop < NZ // 2):
            send(("label", hop, way), labrow.at[(-way * (hop - 1)) % NZ], labrow.at[(-way * hop) % NZ],
                 z_up if way > 0 else z_down)

    def z_arrived(hop, way, chunk):
        arrived(("z", hop, way, chunk), image_slot(-way * hop, chunk), z_up)
        if chunk == (A if way > 0 else B) and (way > 0 or hop < NZ // 2):
            arrived(("label", hop, way), labrow.at[(-way * hop) % NZ], z_up)

    def z_pass(hop, way, chunk):
        z_arrived(hop, way, chunk)
        if hop < NZ // 2 - 1 or (hop == NZ // 2 - 1 and chunk == (A if way > 0 else B)):
            z_send(hop + 1, way, chunk)

    def x_send(what, chunk):
        src, peer = {NEAR: (OWN, near), FAR: (OWN, far), OPPOSITE: (NEAR, far) if chunk == A else (FAR, near)}[what]
        send(("x", what, chunk), x_slot(0, src, chunk), x_slot(0, what, chunk), peer)

    def twin_send(what, chunk):
        send(("twin", what, chunk), x_slot(0, what, chunk), x_slot(1, what, chunk), twin)

    def x_pass(what, chunk):
        arrived(("x", what, chunk), x_slot(0, what, chunk), near)
        if what == (NEAR if chunk == A else FAR):
            x_send(OPPOSITE, chunk)
        twin_send(what, chunk)

    def y_send(hop, way, p, chunk):
        send(("y", hop, way, p, chunk), text_slot(-way * (hop - 1), p, chunk), text_slot(-way * hop, p, chunk),
             y_up if way > 0 else y_down)

    def y_pass(hop, way, p, chunk):
        arrived(("y", hop, way, p, chunk), text_slot(-way * hop, p, chunk), y_up)
        if hop == 1 and chunk == (A if way > 0 else B):
            y_send(2, way, p, chunk)

    def choose(p, chunk):
        target = partner_ref[group]
        same_side, same_core = target // 2 == x_lo, target % 2 == core
        here, there = (OWN, NEAR) if p == 0 else (OPPOSITE, FAR)
        for what in (here, there):
            arrived(("twin", what, chunk), x_slot(1, what, chunk), twin)
        here, there = (jnp.where(same_core, xbuf[0, what, part(chunk)], xbuf[1, what, part(chunk)])
                       for what in (here, there))
        tbuf[pl.ds(text_at(0, p, chunk), half), :] = jnp.where(same_side, here, there)
        y_send(1, 1, p, chunk)
        y_send(1, -1, p, chunk)

    local[0].wait()
    x_send(NEAR, A)
    x_send(FAR, A)
    local[1].wait()
    local[2].wait()
    labrow[0] = jnp.zeros((8, LANES), jnp.int32)
    labrow[0, 0:1, 0:rows] = lab_own[...]
    z_send(1, 1, A)
    z_send(1, -1, B)
    twin_send(OWN, A)
    twin_send(OWN, B)
    x_send(NEAR, B)
    x_send(FAR, B)
    z_send(1, 1, B)
    z_send(1, -1, A)
    for copy in local[3:]:
        copy.wait()

    temper = jnp.exp(jnp.full((1, LANES), temp_ref[0], jnp.float32))
    offset = jnp.full((1, LANES), bias_ref[0], jnp.float32)
    loss_acc[0] = jnp.zeros((8, LANES), jnp.float32)
    n_i, n_t = NZ * rows, 2 * NY * rows

    def label_columns(rels):
        for rel in rels:
            column = jnp.broadcast_to(labrow[rel, 0:1, :], (LANES, LANES)).T
            labcol[image_at(rel):image_at(rel) + rows, :] = column[:rows]

    def slope_quarter(i_half, p):
        left = p * NY * rows
        wide = NY * rows

        def step(k, carry):
            top = pl.multiple_of(i_half * (n_i // 2) + k * LANES, LANES)
            dots = lax.dot_general(ibuf[pl.ds(top, LANES), :], tbuf[left:left + wide, :], (((1,), (1,)), ((), ())),
                                   preferred_element_type=jnp.float32)
            for at in range(0, wide, LANES):
                logits = temper * dots[:, at:at + LANES] + offset
                column = lax.broadcasted_iota(jnp.int32, (1, LANES), 1) + at
                own = column + ((z * (NX // 2) + (x_hi + p) % 2) * NY + y) * rows
                for b in range(1, NY):
                    owner = (z * (NX // 2) + (x_hi + p) % 2) * NY + (y + b) % NY
                    own = jnp.where(column >= b * rows, column + (owner - b) * rows, own)
                hit = labcol[pl.ds(top, LANES), :] == own
                margin = jnp.where(hit, -logits, logits)
                small = jnp.exp(-jnp.abs(logits))
                base = 1.0 + small
                inverse = 1.0 / base
                log_part = jnp.log(base) + (small - (base - 1.0)) * inverse
                loss = jnp.maximum(margin, 0.0) + log_part
                loss_acc[0] += jnp.sum(loss.reshape(LANES // 8, 8, LANES), axis=0)
                slope = jnp.where(margin >= 0.0, 1.0, small) * inverse
                slope = jnp.where(hit, -slope, slope).astype(jnp.bfloat16)
                slopes[pl.ds(top, LANES), left + at:left + at + LANES] = slope
                slopes_t[left + at:left + at + LANES, pl.ds(top, LANES)] = slope.T
            return carry

        lax.fori_loop(0, n_i // 2 // LANES, step, 0)

    x_pass(NEAR, A)
    x_pass(FAR, A)
    z_pass(1, 1, A)
    z_pass(1, -1, B)
    choose(0, A)
    x_pass(NEAR, B)
    x_pass(FAR, B)
    z_pass(1, 1, B)
    z_pass(1, -1, A)
    choose(0, B)
    y_pass(1, 1, 0, A)
    y_pass(1, -1, 0, A)
    x_pass(OPPOSITE, A)
    x_pass(OPPOSITE, B)
    z_pass(2, 1, A)
    z_pass(2, -1, B)
    choose(1, A)
    y_pass(1, 1, 0, B)
    y_pass(1, -1, 0, B)
    choose(1, B)
    z_pass(2, 1, B)
    z_pass(2, -1, A)
    label_columns((0, 1, 7, 2))
    y_pass(2, 1, 0, A)
    y_pass(2, -1, 0, B)
    slope_quarter(0, 0)
    z_pass(3, 1, A)
    z_pass(3, -1, B)
    y_pass(1, 1, 1, A)
    y_pass(1, -1, 1, A)
    y_pass(1, 1, 1, B)
    y_pass(1, -1, 1, B)
    z_pass(3, 1, B)
    z_pass(3, -1, A)
    y_pass(2, 1, 1, A)
    y_pass(2, -1, 1, B)
    slope_quarter(0, 1)
    z_pass(4, 1, A)
    z_pass(4, -1, B)
    label_columns((6, 3, 5, 4))
    slope_quarter(1, 0)
    slope_quarter(1, 1)

    def grad_images(first, count):
        gi[first * rows:(first + count) * rows, :] = jnp.dot(
            slopes[first * rows:(first + count) * rows, :], tbuf[...], preferred_element_type=jnp.float32)

    def grad_texts(first, count):
        gt[first * rows:(first + count) * rows, :] = jnp.dot(
            slopes_t[first * rows:(first + count) * rows, :], ibuf[...], preferred_element_type=jnp.float32)

    def packed(out, value):
        tops = jnp.max(jnp.abs(value).reshape(half // SCALE_ROWS, SCALE_ROWS, width), axis=0)
        top = tops[:, 0:LANES]
        for t in range(1, tiles):
            top = jnp.maximum(top, tops[:, t * LANES:(t + 1) * LANES])
        exponent = jnp.ceil(jnp.log2(jnp.maximum(top, 1e-30)))
        inverse = jnp.concatenate([jnp.exp2(TOP - exponent)] * (half // SCALE_ROWS), axis=0)
        out[tiles * half:tiles * half + SCALE_ROWS, :] = exponent.astype(jnp.int16)
        for t in range(tiles):
            scaled = jnp.round(value[:, t * LANES:(t + 1) * LANES] * inverse)
            out[t * half:(t + 1) * half, :] = scaled.astype(jnp.int32).astype(jnp.int16)

    def unpacked(message):
        exponent = message[tiles * half:tiles * half + SCALE_ROWS, :].astype(jnp.int32).astype(jnp.float32)
        scale = jnp.concatenate([jnp.exp2(exponent - TOP)] * (half // SCALE_ROWS), axis=0)
        return jnp.concatenate(
            [message[t * half:(t + 1) * half, :].astype(jnp.int32).astype(jnp.float32) * scale for t in range(tiles)],
            axis=1)

    def ring(kind, n, out, inbox, up, down, partial):
        halfway = n // 2

        def slot(hop, way, chunk):
            return (0 if way > 0 else 1), 2 * (hop - 1) + chunk

        def get(hop, way, chunk):
            box = inbox.at[slot(hop, way, chunk)]
            arrived((kind, hop, way, chunk), box, up)
            return unpacked(box)

        def put(hop, way, chunk):
            value = partial(way * (halfway + 1 - hop), chunk)
            fresh = hop == 1 or (hop == 2 and chunk == (B if way > 0 else A))
            if not fresh:
                value = value + get(hop - 1, way, chunk)
            at = slot(hop, way, chunk)
            packed(out.at[at], value)
            send((kind, hop, way, chunk), out.at[at], inbox.at[at], up if way > 0 else down)

        def last(chunk):
            return partial(0, chunk) + get(halfway, 1, chunk) + get(halfway, -1, chunk)

        return put, last

    z_put, z_last = ring("gz", NZ, zq_out, zq_in, z_up, z_down,
                         lambda rel, chunk: gi[image_at(rel, chunk):image_at(rel, chunk) + half, :])
    y_puts, y_lasts = [], []
    for p in (0, 1):
        put, last = ring(("gy", p), NY, yq_out.at[p], yq_in.at[p], y_up, y_down,
                         lambda rel, chunk, p=p: gt[text_at(rel, p, chunk):text_at(rel, p, chunk) + half, :])
        y_puts.append(put)
        y_lasts.append(last)

    loss_stages = [(1, core, [(1, twin)]), (NX, x, x_others), (NY, y, y_others), (NZ, z, z_others)]

    def loss_send(stage):
        _, at, others = loss_stages[stage]
        loss_in[stage, at] = loss_acc[stage]
        for d, peer in others:
            send(("loss", stage, d), loss_acc.at[stage], loss_in.at[stage, at], peer)

    def loss_get(stage):
        _, at, others = loss_stages[stage]
        for d, peer in others:
            arrived(("loss", stage, d), loss_in.at[stage, at], peer)
        total = loss_in[stage, 0]
        for k in range(1, len(others) + 1):
            total = total + loss_in[stage, k]
        loss_acc[stage + 1] = total

    def y_finish(p, chunk):
        tsum[p, part(chunk)] = y_lasts[p](chunk)
        packed(sq_out.at[p, chunk], tsum[p, part(chunk)])
        send(("gs", p, chunk), sq_out.at[p, chunk], sq_in.at[p, chunk], twin)

    def twin_get(p, chunk):
        arrived(("gs", p, chunk), sq_in.at[p, chunk], twin)

    def weight(who, home):
        return jnp.full((1, LANES), jnp.where(partner_ref[who] == home, 1.0, 0.0), jnp.float32)

    twin_group, across = x_lo * 2 + (1 - core), (1 - x_lo) * 2 + core
    here_weights = weight(group, group), weight(twin_group, group)
    there_weights = weight(group, across), weight(twin_group, across)

    def x_partial(what, chunk):
        p, (own_weight, twin_weight) = {
            OWN: (0, here_weights), NEAR: (0, there_weights), FAR: (1, there_weights), OPPOSITE: (1, here_weights)}[what]
        own, other = tsum[p, part(chunk)], unpacked(sq_in.at[p, chunk])
        return jnp.concatenate(
            [own[:, t * LANES:(t + 1) * LANES] * own_weight + other[:, t * LANES:(t + 1) * LANES] * twin_weight
             for t in range(tiles)], axis=1)

    def x_get(what, chunk):
        arrived(("gx", what, chunk), xq_in.at[what, chunk], near)
        return unpacked(xq_in.at[what, chunk])

    def x_put(what, chunk):
        value = x_partial(what, chunk)
        if what == (FAR if chunk == A else NEAR):
            value = value + x_get(OPPOSITE, chunk)
        packed(xq_out.at[what, chunk], value)
        peer = {NEAR: near, FAR: far, OPPOSITE: near if chunk == A else far}[what]
        send(("gx", what, chunk), xq_out.at[what, chunk], xq_in.at[what, chunk], peer)

    def write(out, chunk, value):
        for t in range(tiles):
            out[0, part(chunk), t * LANES:(t + 1) * LANES] = temper * value[:, t * LANES:(t + 1) * LANES]

    loss_send(0)
    grad_texts(4, 4)
    y_puts[1](1, 1, A)
    y_puts[1](1, -1, B)
    y_puts[1](2, 1, B)
    y_puts[1](2, -1, A)
    grad_images(5, 3)
    z_put(1, 1, A)
    z_put(1, -1, B)
    z_put(2, 1, B)
    z_put(2, -1, A)
    loss_get(0)
    loss_send(1)
    grad_texts(0, 4)
    y_puts[0](1, 1, A)
    y_puts[0](1, -1, B)
    grad_images(0, 5)
    y_puts[1](2, 1, A)
    y_puts[1](2, -1, B)
    z_put(2, 1, A)
    z_put(2, -1, B)
    z_put(3, 1, B)
    z_put(3, -1, A)
    y_puts[0](2, 1, A)
    y_puts[0](2, -1, A)
    y_puts[0](2, 1, B)
    y_puts[0](2, -1, B)
    loss_get(1)
    loss_send(2)
    z_put(3, 1, A)
    z_put(3, -1, B)
    y_finish(1, A)
    y_finish(1, B)
    z_put(4, 1, B)
    z_put(4, -1, A)
    twin_get(1, A)
    x_put(OPPOSITE, A)
    twin_get(1, B)
    x_put(OPPOSITE, B)
    x_put(FAR, B)
    loss_get(2)
    loss_send(3)
    y_finish(0, A)
    z_put(4, 1, A)
    z_put(4, -1, B)
    twin_get(0, A)
    x_put(NEAR, A)
    x_put(FAR, A)
    y_finish(0, B)
    twin_get(0, B)
    x_put(NEAR, B)
    loss_get(3)
    loss_out[0] = jnp.sum(loss_acc[4]) / total_pairs
    for chunk in (A, B):
        write(img_out, chunk, z_last(chunk))
    for chunk in (A, B):
        write(txt_out, chunk, x_partial(OWN, chunk) + x_get(NEAR, chunk) + x_get(FAR, chunk))
    for copy in pending:
        copy.wait_send()


def shards(image_embeds, text_embeds, positives, partner, log_temp, bias):
    _, rows, width = image_embeds.shape
    half, tiles = rows // 2, width // LANES
    message = (tiles * half + SCALE_ROWS, LANES)
    n_i, n_t = NZ * rows, 2 * NY * rows
    cycle, groups = lax.axis_size("blk"), lax.axis_size("group")
    total_pairs = groups * rows * cycle * cycle
    vmem = pl.BlockSpec(memory_space=pltpu.VMEM)
    smem = pl.BlockSpec(memory_space=pltpu.SMEM)
    anywhere = pl.BlockSpec(memory_space=pl.ANY)
    f32, bf16, i16, i32 = jnp.float32, jnp.bfloat16, jnp.int16, jnp.int32
    copies = 112
    return pl.pallas_call(
        functools.partial(kernel, float(total_pairs)),
        out_shape=(jax.ShapeDtypeStruct((1, rows, width), f32), jax.ShapeDtypeStruct((1, rows, width), f32),
                   jax.ShapeDtypeStruct((1,), f32)),
        in_specs=[anywhere] * 6,
        out_specs=(vmem, vmem, smem),
        scratch_shapes=[
            pltpu.SMEM(partner.shape, i32),
            pltpu.SMEM((1,), f32),
            pltpu.SMEM((1,), f32),
            pltpu.VMEM((1, rows), i32),
            pltpu.VMEM((n_i, width), bf16),
            pltpu.VMEM((n_t, width), bf16),
            pltpu.VMEM((2, NX, rows, width), bf16),
            pltpu.VMEM((NZ, 8, LANES), i32),
            pltpu.VMEM((n_i, LANES), i32),
            pltpu.VMEM((n_i, n_t), bf16),
            pltpu.VMEM((n_t, n_i), bf16),
            pltpu.VMEM((n_i, width), f32),
            pltpu.VMEM((n_t, width), f32),
            pltpu.VMEM((2, rows, width), f32),
            pltpu.VMEM((5, 8, LANES), f32),
            pltpu.VMEM((4, NZ, 8, LANES), f32),
            pltpu.VMEM((2, NZ, *message), i16),
            pltpu.VMEM((2, NZ, *message), i16),
            pltpu.VMEM((2, 2, NY, *message), i16),
            pltpu.VMEM((2, 2, NY, *message), i16),
            pltpu.VMEM((2, 2, *message), i16),
            pltpu.VMEM((2, 2, *message), i16),
            pltpu.VMEM((NX, 2, *message), i16),
            pltpu.VMEM((NX, 2, *message), i16),
            pltpu.SemaphoreType.DMA((copies,)),
            pltpu.SemaphoreType.DMA((copies,)),
            pltpu.SemaphoreType.DMA((6,)),
        ],
        compiler_params=pltpu.CompilerParams(
            collective_id=0, has_side_effects=True, vmem_limit_bytes=48 * 1024 * 1024),
    )(partner, log_temp, bias, image_embeds, text_embeds, positives)


def solution(mesh):
    in_specs = (P("group", "blk", None), P("group", "blk", None), P("group", "blk"), P(), P(), P())
    out_specs = (P("group", "blk", None), P("group", "blk", None), P())
    return jax.shard_map(shards, mesh=mesh, in_specs=in_specs, out_specs=out_specs, check_vma=False)
```

```python
import functools

import jax
import jax.numpy as jnp
from jax import lax
from jax.experimental import pallas as pl
from jax.experimental.pallas import tpu as pltpu
from jax.sharding import PartitionSpec as P

NZ, NX, NY = 8, 4, 4
LANES = 128
PIECES = 6
SCALE_ROWS = 16
TOP = 14.9657842846620869


def kernel(total_pairs, partner_in, temp_in, bias_in, img_in, txt_in, lab_in,
           img_out, txt_out, loss_out,
           partner_ref, temp_ref, bias_ref, lab_own, ibuf, tbuf, xbuf, labrow, labcol, slopes, slopes_t, gi, gt, tsum,
           loss_acc, loss_in, zq_out, zq_in, yq_out, yq_in, sq_out, sq_in, xq_out, xq_in,
           send_sems, recv_sems, local_sems):
    rows, width = img_in.shape[1], img_in.shape[2]
    half, piece = rows // 2, rows // PIECES
    tiles = width // LANES
    A, B = 0, 1
    OWN, NEAR, FAR, OPPOSITE = 0, 1, 2, 3

    local = [pltpu.make_async_copy(src, dst, local_sems.at[k]) for k, (src, dst) in enumerate((
        (txt_in.at[0], xbuf.at[0, OWN]), (img_in.at[0], ibuf.at[0:rows]), (lab_in, lab_own),
        (partner_in, partner_ref), (temp_in, temp_ref), (bias_in, bias_ref)))]
    for copy in local:
        copy.start()

    blk, group = lax.axis_index("blk"), lax.axis_index("group")
    z, x_hi, y = blk // (NX // 2 * NY), (blk // NY) % (NX // 2), blk % NY
    x_lo, core = group // 2, group % 2
    x = x_hi * 2 + x_lo

    def device(z_at, x_at, y_at, core_at):
        return ((z_at % NZ) * (NX // 2 * NY) + ((x_at % NX) // 2) * NY + y_at % NY, (x_at % 2) * 2 + core_at)

    z_up, z_down = device(z + 1, x, y, core), device(z + NZ - 1, x, y, core)
    y_up, y_down = device(z, x, y + 1, core), device(z, x, y + NY - 1, core)
    near, far = device(z, x + 1 + 2 * x_lo, y, core), device(z, x + 3 - 2 * x_lo, y, core)
    twin = device(z, x, y, 1 - core)
    x_others = [(d, device(z, x + d, y, core)) for d in range(1, NX)]
    y_others = [(d, device(z, x, y + d, core)) for d in range(1, NY)]
    z_others = [(d, device(z + d, x, y, core)) for d in range(1, NZ)]

    greeted = [twin] + [peer for _, peer in x_others + y_others + z_others]
    barrier = pltpu.get_barrier_semaphore()
    for peer in greeted:
        pl.semaphore_signal(barrier, inc=1, device_id=peer, device_id_type=pl.DeviceIdType.MESH)
    pl.semaphore_wait(barrier, len(greeted))

    places, pending = {}, []

    def copy_of(name, src, dst, peer):
        place = places.setdefault(name, len(places))
        return pltpu.make_async_remote_copy(
            src_ref=src, dst_ref=dst, send_sem=send_sems.at[place], recv_sem=recv_sems.at[place],
            device_id=peer, device_id_type=pl.DeviceIdType.MESH)

    def send(name, src, dst, peer):
        copy = copy_of(name, src, dst, peer)
        copy.start()
        pending.append(copy)

    def arrived(name, dst, peer):
        copy_of(name, dst, dst, peer).wait_recv()

    def part(chunk):
        return pl.ds(chunk * half, half)

    order, text_order = (0, 1, 7, 2, 6, 3, 5, 4), (0, 1, 3, 2)

    def image_at(rel, chunk=0):
        return order.index(rel % NZ) * rows + chunk * half

    def text_at(rel, p, chunk=0):
        return (p * NY + text_order.index(rel % NY)) * rows + chunk * half

    def image_slot(rel, chunk):
        return ibuf.at[pl.ds(image_at(rel, chunk), half)]

    def text_slot(rel, p, k):
        return tbuf.at[pl.ds(text_at(rel, p) + k * piece, piece)]

    def x_slot(side, which, k):
        return xbuf.at[side, which, pl.ds(k * piece, piece)]

    def low(k):
        return k < PIECES // 2

    def z_send(hop, way, chunk):
        source = img_in.at[0, part(chunk)] if hop == 1 else image_slot(-way * (hop - 1), chunk)
        send(("z", hop, way, chunk), source, image_slot(-way * hop, chunk), z_up if way > 0 else z_down)
        if chunk == (A if way > 0 else B) and (way > 0 or hop < NZ // 2):
            send(("label", hop, way), labrow.at[(-way * (hop - 1)) % NZ], labrow.at[(-way * hop) % NZ],
                 z_up if way > 0 else z_down)

    def z_arrived(hop, way, chunk):
        arrived(("z", hop, way, chunk), image_slot(-way * hop, chunk), z_up)
        if chunk == (A if way > 0 else B) and (way > 0 or hop < NZ // 2):
            arrived(("label", hop, way), labrow.at[(-way * hop) % NZ], z_up)

    def z_pass(hop, way, chunk):
        z_arrived(hop, way, chunk)
        if hop < NZ // 2 - 1 or (hop == NZ // 2 - 1 and chunk == (A if way > 0 else B)):
            z_send(hop + 1, way, chunk)

    def x_send(what, k):
        src, peer = {NEAR: (OWN, near), FAR: (OWN, far), OPPOSITE: (NEAR, far) if low(k) else (FAR, near)}[what]
        source = txt_in.at[0, pl.ds(k * piece, piece)] if src == OWN else x_slot(0, src, k)
        send(("x", what, k), source, x_slot(0, what, k), peer)

    def twin_send(what, k):
        source = txt_in.at[0, pl.ds(k * piece, piece)] if what == OWN else x_slot(0, what, k)
        send(("twin", what, k), source, x_slot(1, what, k), twin)

    def x_pass(what, k):
        arrived(("x", what, k), x_slot(0, what, k), near)
        if what == (NEAR if low(k) else FAR):
            x_send(OPPOSITE, k)
        twin_send(what, k)

    def y_send(hop, way, p, k):
        send(("y", hop, way, p, k), text_slot(-way * (hop - 1), p, k), text_slot(-way * hop, p, k),
             y_up if way > 0 else y_down)

    def y_pass(hop, way, p, k):
        arrived(("y", hop, way, p, k), text_slot(-way * hop, p, k), y_up)
        if hop == 1 and low(k) == (way > 0):
            y_send(2, way, p, k)

    def choose(p, k):
        target = partner_ref[group]
        same_side, same_core = target // 2 == x_lo, target % 2 == core
        here, there = (OWN, NEAR) if p == 0 else (OPPOSITE, FAR)
        for what in (here, there):
            arrived(("twin", what, k), x_slot(1, what, k), twin)
        here, there = (jnp.where(same_core, xbuf[0, what, pl.ds(k * piece, piece)], xbuf[1, what, pl.ds(k * piece, piece)])
                       for what in (here, there))
        tbuf[pl.ds(text_at(0, p) + k * piece, piece), :] = jnp.where(same_side, here, there)

    x_send(NEAR, 0)
    x_send(FAR, 3)
    twin_send(OWN, 0)
    local[2].wait()
    labrow[0] = jnp.zeros((8, LANES), jnp.int32)
    labrow[0, 0:1, 0:rows] = lab_own[...]
    z_send(1, 1, A)
    z_send(1, -1, B)
    z_send(1, 1, B)
    z_send(1, -1, A)
    x_send(NEAR, 1)
    x_send(FAR, 4)
    twin_send(OWN, 1)
    x_send(NEAR, 2)
    x_send(FAR, 5)
    twin_send(OWN, 2)
    x_send(NEAR, 3)
    x_send(FAR, 0)
    twin_send(OWN, 3)
    x_send(NEAR, 4)
    x_send(FAR, 1)
    twin_send(OWN, 4)
    x_send(NEAR, 5)
    x_send(FAR, 2)
    twin_send(OWN, 5)
    for copy in local[:2] + local[3:]:
        copy.wait()

    temper = jnp.exp(jnp.full((1, LANES), temp_ref[0], jnp.float32))
    offset = jnp.full((1, LANES), bias_ref[0], jnp.float32)
    loss_acc[0] = jnp.zeros((8, LANES), jnp.float32)
    n_i, n_t = NZ * rows, 2 * NY * rows

    def label_columns(rels):
        for rel in rels:
            column = jnp.broadcast_to(labrow[rel, 0:1, :], (LANES, LANES)).T
            labcol[image_at(rel):image_at(rel) + rows, :] = column[:rows]

    def slope_tiles(first, count, left, right):
        wide = 2 * LANES
        blocks = [(p, rel) for p in (0, 1) for rel in text_order]

        def text_rows(at):
            column = lax.broadcasted_iota(jnp.int32, (1, LANES), 1) + at
            found = column
            for b, (p, rel) in enumerate(blocks):
                owner = (z * (NX // 2) + (x_hi + p) % 2) * NY + (y + rel) % NY
                found = jnp.where(column >= b * rows, column + (owner - b) * rows, found)
            return found

        def step(k, carry):
            top = pl.multiple_of(k * wide, wide)
            for start in range(left, right, wide):
                stop = min(start + wide, right)
                dots = lax.dot_general(ibuf[pl.ds(top, wide), :], tbuf[start:stop, :], (((1,), (1,)), ((), ())),
                                       preferred_element_type=jnp.float32)
                for at in range(start, stop, LANES):
                    logits = temper * dots[:, at - start:at - start + LANES] + offset
                    hit = labcol[pl.ds(top, wide), :] == text_rows(at)
                    margin = jnp.where(hit, -logits, logits)
                    small = jnp.exp(-jnp.abs(logits))
                    base = 1.0 + small
                    inverse = 1.0 / base
                    log_part = jnp.log(base) + (small - (base - 1.0)) * inverse
                    loss = jnp.maximum(margin, 0.0) + log_part
                    loss_acc[0] += jnp.sum(loss.reshape(wide // 8, 8, LANES), axis=0)
                    slope = jnp.where(margin >= 0.0, 1.0, small) * inverse
                    slope = jnp.where(hit, -slope, slope).astype(jnp.bfloat16)
                    slopes[pl.ds(top, wide), at:at + LANES] = slope
                    slopes_t[at:at + LANES, pl.ds(top, wide)] = slope.T
            return carry

        lax.fori_loop(first, first + count, step, 0)

    x_pass(NEAR, 0)
    x_pass(FAR, 3)
    x_pass(NEAR, 1)
    x_pass(FAR, 4)
    choose(0, 0)
    y_send(1, 1, 0, 0)
    y_send(1, -1, 0, 0)
    x_pass(NEAR, 2)
    x_pass(FAR, 5)
    z_pass(1, 1, A)
    z_pass(1, -1, B)
    choose(0, 1)
    y_send(1, 1, 0, 1)
    y_send(1, -1, 0, 1)
    x_pass(NEAR, 3)
    x_pass(FAR, 0)
    choose(0, 2)
    y_send(1, 1, 0, 2)
    y_send(1, -1, 0, 2)
    x_pass(NEAR, 4)
    x_pass(FAR, 1)
    choose(0, 3)
    y_send(1, -1, 0, 3)
    y_send(1, 1, 0, 3)
    x_pass(NEAR, 5)
    x_pass(FAR, 2)
    z_pass(1, 1, B)
    z_pass(1, -1, A)
    y_pass(1, 1, 0, 0)
    y_pass(1, -1, 0, 0)
    choose(0, 4)
    y_send(1, -1, 0, 4)
    y_send(1, 1, 0, 4)
    x_pass(OPPOSITE, 3)
    x_pass(OPPOSITE, 0)
    y_pass(1, 1, 0, 1)
    y_pass(1, -1, 0, 1)
    choose(0, 5)
    y_send(1, -1, 0, 5)
    y_send(1, 1, 0, 5)
    x_pass(OPPOSITE, 4)
    x_pass(OPPOSITE, 1)
    y_pass(1, 1, 0, 2)
    y_pass(1, -1, 0, 2)
    choose(1, 3)
    y_send(1, -1, 1, 3)
    choose(1, 0)
    y_send(1, 1, 1, 0)
    x_pass(OPPOSITE, 5)
    x_pass(OPPOSITE, 2)
    z_pass(2, 1, A)
    z_pass(2, -1, B)
    y_pass(1, 1, 0, 3)
    y_pass(1, -1, 0, 3)
    choose(1, 4)
    y_send(1, -1, 1, 4)
    choose(1, 1)
    y_send(1, 1, 1, 1)
    y_pass(2, 1, 0, 0)
    y_pass(1, -1, 0, 4)
    choose(1, 5)
    y_send(1, -1, 1, 5)
    choose(1, 2)
    y_send(1, 1, 1, 2)
    y_pass(1, 1, 0, 4)
    y_pass(1, -1, 0, 5)
    y_send(1, 1, 1, 3)
    y_send(1, -1, 1, 0)
    y_send(1, 1, 1, 4)
    y_send(1, -1, 1, 1)
    y_send(1, 1, 1, 5)
    y_send(1, -1, 1, 2)
    z_pass(2, 1, B)
    z_pass(2, -1, A)
    label_columns((0, 1, 7, 2))
    y_pass(2, 1, 0, 1)
    y_pass(1, -1, 1, 3)
    y_pass(1, 1, 0, 5)
    y_pass(2, -1, 0, 3)
    y_pass(2, 1, 0, 2)
    y_pass(1, -1, 1, 4)
    z_pass(3, 1, A)
    z_pass(3, -1, B)
    y_pass(1, 1, 1, 0)
    y_pass(2, -1, 0, 4)
    y_pass(1, 1, 1, 1)
    y_pass(1, -1, 1, 5)
    y_pass(1, 1, 1, 2)
    y_pass(2, -1, 0, 5)
    z_pass(3, 1, B)
    z_pass(3, -1, A)
    label_columns((6, 3, 5))
    slope_tiles(0, 2, 0, 3 * LANES)
    y_pass(1, 1, 1, 3)
    y_pass(1, -1, 1, 0)
    y_pass(1, 1, 1, 4)
    y_pass(1, -1, 1, 1)
    y_pass(1, 1, 1, 5)
    y_pass(1, -1, 1, 2)
    z_pass(4, 1, A)
    z_pass(4, -1, B)
    label_columns((4,))
    slope_tiles(2, 1, 0, 3 * LANES)
    slope_tiles(0, 3, 3 * LANES, 5 * LANES)
    y_pass(2, 1, 1, 0)
    y_pass(2, -1, 1, 3)
    y_pass(2, 1, 1, 1)
    y_pass(2, -1, 1, 4)
    y_pass(2, 1, 1, 2)
    y_pass(2, -1, 1, 5)
    slope_tiles(0, 3, 5 * LANES, 6 * LANES)

    def grad_images(first, count):
        gi[first * rows:(first + count) * rows, :] = jnp.dot(
            slopes[first * rows:(first + count) * rows, :], tbuf[...], preferred_element_type=jnp.float32)

    def grad_texts(first, count):
        gt[first * rows:(first + count) * rows, :] = jnp.dot(
            slopes_t[first * rows:(first + count) * rows, :], ibuf[...], preferred_element_type=jnp.float32)

    def packed(out, value):
        tops = jnp.max(jnp.abs(value).reshape(half // SCALE_ROWS, SCALE_ROWS, width), axis=0)
        top = tops[:, 0:LANES]
        for t in range(1, tiles):
            top = jnp.maximum(top, tops[:, t * LANES:(t + 1) * LANES])
        exponent = jnp.ceil(jnp.log2(jnp.maximum(top, 1e-30)))
        inverse = jnp.concatenate([jnp.exp2(TOP - exponent)] * (half // SCALE_ROWS), axis=0)
        out[tiles * half:tiles * half + SCALE_ROWS, :] = exponent.astype(jnp.int16)
        for t in range(tiles):
            scaled = jnp.round(value[:, t * LANES:(t + 1) * LANES] * inverse)
            out[t * half:(t + 1) * half, :] = scaled.astype(jnp.int32).astype(jnp.int16)

    def unpacked(message):
        exponent = message[tiles * half:tiles * half + SCALE_ROWS, :].astype(jnp.int32).astype(jnp.float32)
        scale = jnp.concatenate([jnp.exp2(exponent - TOP)] * (half // SCALE_ROWS), axis=0)
        return jnp.concatenate(
            [message[t * half:(t + 1) * half, :].astype(jnp.int32).astype(jnp.float32) * scale for t in range(tiles)],
            axis=1)

    def ring(kind, n, out, inbox, up, down, partial):
        halfway = n // 2

        def slot(hop, way, chunk):
            return (0 if way > 0 else 1), 2 * (hop - 1) + chunk

        def get(hop, way, chunk):
            box = inbox.at[slot(hop, way, chunk)]
            arrived((kind, hop, way, chunk), box, up)
            return unpacked(box)

        def put(hop, way, chunk):
            value = partial(way * (halfway + 1 - hop), chunk)
            fresh = hop == 1 or (hop == 2 and chunk == (B if way > 0 else A))
            if not fresh:
                value = value + get(hop - 1, way, chunk)
            at = slot(hop, way, chunk)
            packed(out.at[at], value)
            send((kind, hop, way, chunk), out.at[at], inbox.at[at], up if way > 0 else down)

        def last(chunk):
            return partial(0, chunk) + get(halfway, 1, chunk) + get(halfway, -1, chunk)

        return put, last

    z_put, z_last = ring("gz", NZ, zq_out, zq_in, z_up, z_down,
                         lambda rel, chunk: gi[image_at(rel, chunk):image_at(rel, chunk) + half, :])
    y_puts, y_lasts = [], []
    for p in (0, 1):
        put, last = ring(("gy", p), NY, yq_out.at[p], yq_in.at[p], y_up, y_down,
                         lambda rel, chunk, p=p: gt[text_at(rel, p, chunk):text_at(rel, p, chunk) + half, :])
        y_puts.append(put)
        y_lasts.append(last)

    loss_stages = [(z, z_others), (x, x_others), (core, [(1, twin)]), (y, y_others)]

    def loss_send(stage):
        at, others = loss_stages[stage]
        loss_in[stage, at] = loss_acc[stage]
        for d, peer in others:
            send(("loss", stage, d), loss_acc.at[stage], loss_in.at[stage, at], peer)

    def loss_get(stage):
        at, others = loss_stages[stage]
        for d, peer in others:
            arrived(("loss", stage, d), loss_in.at[stage, at], peer)
        total = loss_in[stage, 0]
        for k in range(1, len(others) + 1):
            total = total + loss_in[stage, k]
        loss_acc[stage + 1] = total

    def y_finish(p, chunk):
        tsum[p, part(chunk)] = y_lasts[p](chunk)
        packed(sq_out.at[p, chunk], tsum[p, part(chunk)])
        send(("gs", p, chunk), sq_out.at[p, chunk], sq_in.at[p, chunk], twin)

    def twin_get(p, chunk):
        arrived(("gs", p, chunk), sq_in.at[p, chunk], twin)

    def weight(who, home):
        return jnp.full((1, LANES), jnp.where(partner_ref[who] == home, 1.0, 0.0), jnp.float32)

    twin_group, across = x_lo * 2 + (1 - core), (1 - x_lo) * 2 + core
    here_weights = weight(group, group), weight(twin_group, group)
    there_weights = weight(group, across), weight(twin_group, across)

    def x_partial(what, chunk):
        p, (own_weight, twin_weight) = {
            OWN: (0, here_weights), NEAR: (0, there_weights), FAR: (1, there_weights), OPPOSITE: (1, here_weights)}[what]
        own, other = tsum[p, part(chunk)], unpacked(sq_in.at[p, chunk])
        return jnp.concatenate(
            [own[:, t * LANES:(t + 1) * LANES] * own_weight + other[:, t * LANES:(t + 1) * LANES] * twin_weight
             for t in range(tiles)], axis=1)

    def x_get(what, chunk):
        arrived(("gx", what, chunk), xq_in.at[what, chunk], near)
        return unpacked(xq_in.at[what, chunk])

    def x_put(what, chunk):
        value = x_partial(what, chunk)
        if what == (FAR if chunk == A else NEAR):
            value = value + x_get(OPPOSITE, chunk)
        packed(xq_out.at[what, chunk], value)
        peer = {NEAR: near, FAR: far, OPPOSITE: near if chunk == A else far}[what]
        send(("gx", what, chunk), xq_out.at[what, chunk], xq_in.at[what, chunk], peer)

    def write(out, chunk, value):
        out[0, part(chunk), :] = value

    loss_send(0)
    grad_texts(7, 1)
    y_puts[1](1, 1, A)
    y_puts[1](1, -1, B)
    grad_texts(3, 1)
    y_puts[0](1, 1, A)
    y_puts[0](1, -1, B)
    grad_images(5, 3)
    z_put(1, 1, A)
    z_put(1, -1, B)
    z_put(2, 1, B)
    z_put(2, -1, A)
    grad_texts(4, 3)
    y_puts[1](2, 1, B)
    y_puts[1](2, -1, A)
    grad_texts(0, 3)
    grad_images(0, 5)
    loss_get(0)
    loss_send(1)
    y_puts[1](2, 1, A)
    y_puts[1](2, -1, B)
    z_put(2, 1, A)
    z_put(2, -1, B)
    y_puts[0](2, 1, A)
    y_puts[0](2, -1, A)
    y_puts[0](2, -1, B)
    y_puts[0](2, 1, B)
    z_put(3, 1, B)
    z_put(3, -1, A)
    loss_get(1)
    loss_send(2)
    z_put(3, 1, A)
    z_put(3, -1, B)
    y_finish(1, A)
    y_finish(1, B)
    loss_get(2)
    loss_send(3)
    z_put(4, 1, B)
    z_put(4, -1, A)
    twin_get(1, A)
    x_put(OPPOSITE, A)
    twin_get(1, B)
    x_put(OPPOSITE, B)
    x_put(FAR, B)
    y_finish(0, A)
    z_put(4, 1, A)
    z_put(4, -1, B)
    twin_get(0, A)
    x_put(NEAR, A)
    y_finish(0, B)
    x_put(FAR, A)
    twin_get(0, B)
    x_put(NEAR, B)
    loss_get(3)
    loss_out[0] = jnp.sum(loss_acc[4]) / total_pairs
    for chunk in (A, B):
        write(img_out, chunk, z_last(chunk))
    for chunk in (A, B):
        write(txt_out, chunk, x_partial(OWN, chunk) + x_get(NEAR, chunk) + x_get(FAR, chunk))
    for copy in pending:
        copy.wait_send()


def shards(image_embeds, text_embeds, positives, partner, log_temp, bias):
    _, rows, width = image_embeds.shape
    half, tiles = rows // 2, width // LANES
    message = (tiles * half + SCALE_ROWS, LANES)
    n_i, n_t = NZ * rows, 2 * NY * rows
    cycle, groups = lax.axis_size("blk"), lax.axis_size("group")
    total_pairs = groups * rows * cycle * cycle
    vmem = pl.BlockSpec(memory_space=pltpu.VMEM)
    smem = pl.BlockSpec(memory_space=pltpu.SMEM)
    hbm = pl.BlockSpec(memory_space=pltpu.HBM)
    in_hbm = functools.partial(pltpu.with_memory_space_constraint, memory_space=pltpu.HBM)
    f32, bf16, i16, i32 = jnp.float32, jnp.bfloat16, jnp.int16, jnp.int32
    copies = 176
    images, texts, loss = pl.pallas_call(
        functools.partial(kernel, float(total_pairs)),
        out_shape=(jax.ShapeDtypeStruct((1, rows, width), f32), jax.ShapeDtypeStruct((1, rows, width), f32),
                   jax.ShapeDtypeStruct((1,), f32)),
        in_specs=[hbm] * 6,
        out_specs=(vmem, vmem, smem),
        scratch_shapes=[
            pltpu.SMEM(partner.shape, i32),
            pltpu.SMEM((1,), f32),
            pltpu.SMEM((1,), f32),
            pltpu.VMEM((1, rows), i32),
            pltpu.VMEM((n_i, width), bf16),
            pltpu.VMEM((n_t, width), bf16),
            pltpu.VMEM((2, NX, rows, width), bf16),
            pltpu.VMEM((NZ, 8, LANES), i32),
            pltpu.VMEM((n_i, LANES), i32),
            pltpu.VMEM((n_i, n_t), bf16),
            pltpu.VMEM((n_t, n_i), bf16),
            pltpu.VMEM((n_i, width), f32),
            pltpu.VMEM((n_t, width), f32),
            pltpu.VMEM((2, rows, width), f32),
            pltpu.VMEM((5, 8, LANES), f32),
            pltpu.VMEM((4, NZ, 8, LANES), f32),
            pltpu.VMEM((2, NZ, *message), i16),
            pltpu.VMEM((2, NZ, *message), i16),
            pltpu.VMEM((2, 2, NY, *message), i16),
            pltpu.VMEM((2, 2, NY, *message), i16),
            pltpu.VMEM((2, 2, *message), i16),
            pltpu.VMEM((2, 2, *message), i16),
            pltpu.VMEM((NX, 2, *message), i16),
            pltpu.VMEM((NX, 2, *message), i16),
            pltpu.SemaphoreType.DMA((copies,)),
            pltpu.SemaphoreType.DMA((copies,)),
            pltpu.SemaphoreType.DMA((6,)),
        ],
        compiler_params=pltpu.CompilerParams(
            collective_id=0, has_side_effects=True, vmem_limit_bytes=48 * 1024 * 1024),
    )(in_hbm(partner), log_temp, bias, in_hbm(image_embeds), in_hbm(text_embeds), in_hbm(positives))
    temper = jnp.exp(log_temp[0])
    return temper * images, temper * texts, loss


def solution(mesh):
    in_specs = (P("group", "blk", None), P("group", "blk", None), P("group", "blk"), P(), P(), P())
    out_specs = (P("group", "blk", None), P("group", "blk", None), P())
    return jax.shard_map(shards, mesh=mesh, in_specs=in_specs, out_specs=out_specs, check_vma=False)
```

```python
import functools

import jax
import jax.numpy as jnp
from jax import lax
from jax.experimental import pallas as pl
from jax.experimental.pallas import tpu as pltpu
from jax.sharding import PartitionSpec as P

NZ, NX, NY = 8, 4, 4
LANES = 128
PIECES = 6
SCALE_ROWS = 16
TOP = 14.9657842846620869


def kernel(total_pairs, partner_in, temp_in, bias_in, img_in, txt_in, lab_in,
           img_out, txt_out, loss_out,
           partner_ref, temp_ref, bias_ref, lab_own, ibuf, tbuf, xbuf, labrow, labcol, slopes, slopes_t, gi, gt, tsum,
           loss_acc, loss_in, zq_out, zq_in, yq_out, yq_in, sq_out, sq_in, xq_out, xq_in,
           send_sems, recv_sems, local_sems):
    rows, width = img_in.shape[1], img_in.shape[2]
    half, piece = rows // 2, rows // PIECES
    tiles = width // LANES
    A, B = 0, 1
    OWN, NEAR, FAR, OPPOSITE = 0, 1, 2, 3

    local = [pltpu.make_async_copy(src, dst, local_sems.at[k]) for k, (src, dst) in enumerate((
        (txt_in.at[0], xbuf.at[0, OWN]), (img_in.at[0], ibuf.at[0:rows]), (lab_in, lab_own),
        (partner_in, partner_ref), (temp_in, temp_ref), (bias_in, bias_ref)))]
    for copy in local:
        copy.start()

    blk, group = lax.axis_index("blk"), lax.axis_index("group")
    z, x_hi, y = blk // (NX // 2 * NY), (blk // NY) % (NX // 2), blk % NY
    x_lo, core = group // 2, group % 2
    x = x_hi * 2 + x_lo

    def device(z_at, x_at, y_at, core_at):
        return ((z_at % NZ) * (NX // 2 * NY) + ((x_at % NX) // 2) * NY + y_at % NY, (x_at % 2) * 2 + core_at)

    z_up, z_down = device(z + 1, x, y, core), device(z + NZ - 1, x, y, core)
    y_up, y_down = device(z, x, y + 1, core), device(z, x, y + NY - 1, core)
    near, far = device(z, x + 1 + 2 * x_lo, y, core), device(z, x + 3 - 2 * x_lo, y, core)
    twin = device(z, x, y, 1 - core)
    x_others = [(d, device(z, x + d, y, core)) for d in range(1, NX)]
    y_others = [(d, device(z, x, y + d, core)) for d in range(1, NY)]
    z_others = [(d, device(z + d, x, y, core)) for d in range(1, NZ)]

    greeted = [twin] + [peer for _, peer in x_others + y_others + z_others]
    barrier = pltpu.get_barrier_semaphore()
    for peer in greeted:
        pl.semaphore_signal(barrier, inc=1, device_id=peer, device_id_type=pl.DeviceIdType.MESH)
    pl.semaphore_wait(barrier, len(greeted))

    places, pending = {}, []

    def copy_of(name, src, dst, peer):
        place = places.setdefault(name, len(places))
        return pltpu.make_async_remote_copy(
            src_ref=src, dst_ref=dst, send_sem=send_sems.at[place], recv_sem=recv_sems.at[place],
            device_id=peer, device_id_type=pl.DeviceIdType.MESH)

    def send(name, src, dst, peer):
        copy = copy_of(name, src, dst, peer)
        copy.start()
        pending.append(copy)

    def arrived(name, dst, peer):
        copy_of(name, dst, dst, peer).wait_recv()

    def part(chunk):
        return pl.ds(chunk * half, half)

    order, text_order = (0, 1, 7, 2, 6, 3, 5, 4), (0, 1, 3, 2)

    def image_at(rel, chunk=0):
        return order.index(rel % NZ) * rows + chunk * half

    def text_at(rel, p, chunk=0):
        return (p * NY + text_order.index(rel % NY)) * rows + chunk * half

    def image_slot(rel, chunk):
        return ibuf.at[pl.ds(image_at(rel, chunk), half)]

    def text_slot(rel, p, k):
        return tbuf.at[pl.ds(text_at(rel, p) + k * piece, piece)]

    def x_slot(side, which, k):
        return xbuf.at[side, which, pl.ds(k * piece, piece)]

    def low(k):
        return k < PIECES // 2

    def z_send(hop, way, chunk):
        source = img_in.at[0, part(chunk)] if hop == 1 else image_slot(-way * (hop - 1), chunk)
        send(("z", hop, way, chunk), source, image_slot(-way * hop, chunk), z_up if way > 0 else z_down)
        if hop > 1 and chunk == (A if way > 0 else B) and (way > 0 or hop < NZ // 2):
            label_send(hop, way)

    def label_send(hop, way):
        send(("label", hop, way), labrow.at[(-way * (hop - 1)) % NZ], labrow.at[(-way * hop) % NZ],
             z_up if way > 0 else z_down)

    def z_arrived(hop, way, chunk):
        arrived(("z", hop, way, chunk), image_slot(-way * hop, chunk), z_up)
        if chunk == (A if way > 0 else B) and (way > 0 or hop < NZ // 2):
            arrived(("label", hop, way), labrow.at[(-way * hop) % NZ], z_up)

    def z_pass(hop, way, chunk):
        z_arrived(hop, way, chunk)
        if hop < NZ // 2 - 1 or (hop == NZ // 2 - 1 and chunk == (A if way > 0 else B)):
            z_send(hop + 1, way, chunk)

    def x_send(what, k):
        src, peer = {NEAR: (OWN, near), FAR: (OWN, far), OPPOSITE: (NEAR, far) if low(k) else (FAR, near)}[what]
        source = txt_in.at[0, pl.ds(k * piece, piece)] if src == OWN else x_slot(0, src, k)
        send(("x", what, k), source, x_slot(0, what, k), peer)

    def twin_send(what, k):
        source = txt_in.at[0, pl.ds(k * piece, piece)] if what == OWN else x_slot(0, what, k)
        send(("twin", what, k), source, x_slot(1, what, k), twin)

    def x_pass(what, k):
        arrived(("x", what, k), x_slot(0, what, k), near)
        if what == (NEAR if low(k) else FAR):
            x_send(OPPOSITE, k)
        twin_send(what, k)

    def y_send(hop, way, p, k):
        send(("y", hop, way, p, k), text_slot(-way * (hop - 1), p, k), text_slot(-way * hop, p, k),
             y_up if way > 0 else y_down)

    def y_pass(hop, way, p, k):
        arrived(("y", hop, way, p, k), text_slot(-way * hop, p, k), y_up)
        if hop == 1 and low(k) == (way > 0):
            y_send(2, way, p, k)

    def choose(p, k):
        target = partner_ref[group]
        same_side, same_core = target // 2 == x_lo, target % 2 == core
        here, there = (OWN, NEAR) if p == 0 else (OPPOSITE, FAR)
        for what in (here, there):
            arrived(("twin", what, k), x_slot(1, what, k), twin)
        here, there = (jnp.where(same_core, xbuf[0, what, pl.ds(k * piece, piece)], xbuf[1, what, pl.ds(k * piece, piece)])
                       for what in (here, there))
        tbuf[pl.ds(text_at(0, p) + k * piece, piece), :] = jnp.where(same_side, here, there)

    x_send(NEAR, 0)
    x_send(FAR, 3)
    twin_send(OWN, 0)
    z_send(1, 1, A)
    z_send(1, -1, B)
    z_send(1, 1, B)
    z_send(1, -1, A)
    x_send(NEAR, 1)
    x_send(FAR, 4)
    twin_send(OWN, 1)
    x_send(NEAR, 2)
    x_send(FAR, 5)
    twin_send(OWN, 2)
    x_send(NEAR, 3)
    x_send(FAR, 0)
    twin_send(OWN, 3)
    x_send(NEAR, 4)
    x_send(FAR, 1)
    twin_send(OWN, 4)
    x_send(NEAR, 5)
    x_send(FAR, 2)
    twin_send(OWN, 5)
    local[2].wait()
    labrow[0] = jnp.zeros((8, LANES), jnp.int32)
    labrow[0, 0:1, 0:rows] = lab_own[...]
    label_send(1, 1)
    label_send(1, -1)
    for copy in local[:2] + local[3:]:
        copy.wait()

    temper = jnp.exp(jnp.full((1, LANES), temp_ref[0], jnp.float32))
    offset = jnp.full((1, LANES), bias_ref[0], jnp.float32)
    loss_acc[0] = jnp.zeros((8, LANES), jnp.float32)
    n_i, n_t = NZ * rows, 2 * NY * rows

    def label_columns(rels):
        for rel in rels:
            column = jnp.broadcast_to(labrow[rel, 0:1, :], (LANES, LANES)).T
            labcol[image_at(rel):image_at(rel) + rows, :] = column[:rows]

    def slope_tiles(first, count, left, right):
        wide = 2 * LANES
        blocks = [(p, rel) for p in (0, 1) for rel in text_order]

        def text_rows(at):
            column = lax.broadcasted_iota(jnp.int32, (1, LANES), 1) + at
            found = column
            for b, (p, rel) in enumerate(blocks):
                owner = (z * (NX // 2) + (x_hi + p) % 2) * NY + (y + rel) % NY
                found = jnp.where(column >= b * rows, column + (owner - b) * rows, found)
            return found

        def step(k, carry):
            top = pl.multiple_of(k * wide, wide)
            for start in range(left, right, wide):
                stop = min(start + wide, right)
                dots = lax.dot_general(ibuf[pl.ds(top, wide), :], tbuf[start:stop, :], (((1,), (1,)), ((), ())),
                                       preferred_element_type=jnp.float32)
                for at in range(start, stop, LANES):
                    logits = temper * dots[:, at - start:at - start + LANES] + offset
                    hit = labcol[pl.ds(top, wide), :] == text_rows(at)
                    margin = jnp.where(hit, -logits, logits)
                    small = jnp.exp(-jnp.abs(logits))
                    base = 1.0 + small
                    inverse = 1.0 / base
                    log_part = jnp.log(base) + (small - (base - 1.0)) * inverse
                    loss = jnp.maximum(margin, 0.0) + log_part
                    loss_acc[0] += jnp.sum(loss.reshape(wide // 8, 8, LANES), axis=0)
                    slope = jnp.where(margin >= 0.0, 1.0, small) * inverse
                    slope = jnp.where(hit, -slope, slope).astype(jnp.bfloat16)
                    slopes[pl.ds(top, wide), at:at + LANES] = slope
                    slopes_t[at:at + LANES, pl.ds(top, wide)] = slope.T
            return carry

        lax.fori_loop(first, first + count, step, 0)

    def grad_images(first, count):
        gi[first * rows:(first + count) * rows, :] = jnp.dot(
            slopes[first * rows:(first + count) * rows, :], tbuf[...], preferred_element_type=jnp.float32)

    def grad_texts(first, count):
        gt[first * rows:(first + count) * rows, :] = jnp.dot(
            slopes_t[first * rows:(first + count) * rows, :], ibuf[...], preferred_element_type=jnp.float32)

    def packed(out, value):
        tops = jnp.max(jnp.abs(value).reshape(half // SCALE_ROWS, SCALE_ROWS, width), axis=0)
        top = tops[:, 0:LANES]
        for t in range(1, tiles):
            top = jnp.maximum(top, tops[:, t * LANES:(t + 1) * LANES])
        exponent = jnp.ceil(jnp.log2(jnp.maximum(top, 1e-30)))
        inverse = jnp.concatenate([jnp.exp2(TOP - exponent)] * (half // SCALE_ROWS), axis=0)
        out[tiles * half:tiles * half + SCALE_ROWS, :] = exponent.astype(jnp.int16)
        for t in range(tiles):
            scaled = jnp.round(value[:, t * LANES:(t + 1) * LANES] * inverse)
            out[t * half:(t + 1) * half, :] = scaled.astype(jnp.int32).astype(jnp.int16)

    def unpacked(message):
        exponent = message[tiles * half:tiles * half + SCALE_ROWS, :].astype(jnp.int32).astype(jnp.float32)
        scale = jnp.concatenate([jnp.exp2(exponent - TOP)] * (half // SCALE_ROWS), axis=0)
        return jnp.concatenate(
            [message[t * half:(t + 1) * half, :].astype(jnp.int32).astype(jnp.float32) * scale for t in range(tiles)],
            axis=1)

    def ring(kind, n, out, inbox, up, down, partial):
        halfway = n // 2

        def slot(hop, way, chunk):
            return (0 if way > 0 else 1), 2 * (hop - 1) + chunk

        def get(hop, way, chunk):
            box = inbox.at[slot(hop, way, chunk)]
            arrived((kind, hop, way, chunk), box, up)
            return unpacked(box)

        def put(hop, way, chunk):
            value = partial(way * (halfway + 1 - hop), chunk)
            fresh = hop == 1 or (hop == 2 and chunk == (B if way > 0 else A))
            if not fresh:
                value = value + get(hop - 1, way, chunk)
            at = slot(hop, way, chunk)
            packed(out.at[at], value)
            send((kind, hop, way, chunk), out.at[at], inbox.at[at], up if way > 0 else down)

        def last(chunk):
            return partial(0, chunk) + get(halfway, 1, chunk) + get(halfway, -1, chunk)

        return put, last

    z_put, z_last = ring("gz", NZ, zq_out, zq_in, z_up, z_down,
                         lambda rel, chunk: gi[image_at(rel, chunk):image_at(rel, chunk) + half, :])
    y_puts, y_lasts = [], []
    for p in (0, 1):
        put, last = ring(("gy", p), NY, yq_out.at[p], yq_in.at[p], y_up, y_down,
                         lambda rel, chunk, p=p: gt[text_at(rel, p, chunk):text_at(rel, p, chunk) + half, :])
        y_puts.append(put)
        y_lasts.append(last)

    loss_stages = [(z, z_others), (x, x_others), (core, [(1, twin)]), (y, y_others)]

    def loss_send(stage):
        at, others = loss_stages[stage]
        loss_in[stage, at] = loss_acc[stage]
        for d, peer in others:
            send(("loss", stage, d), loss_acc.at[stage], loss_in.at[stage, at], peer)

    def loss_get(stage):
        at, others = loss_stages[stage]
        for d, peer in others:
            arrived(("loss", stage, d), loss_in.at[stage, at], peer)
        total = loss_in[stage, 0]
        for k in range(1, len(others) + 1):
            total = total + loss_in[stage, k]
        loss_acc[stage + 1] = total

    def y_finish(p, chunk):
        tsum[p, part(chunk)] = y_lasts[p](chunk)
        packed(sq_out.at[p, chunk], tsum[p, part(chunk)])
        send(("gs", p, chunk), sq_out.at[p, chunk], sq_in.at[p, chunk], twin)

    def twin_get(p, chunk):
        arrived(("gs", p, chunk), sq_in.at[p, chunk], twin)

    def weight(who, home):
        return jnp.full((1, LANES), jnp.where(partner_ref[who] == home, 1.0, 0.0), jnp.float32)

    twin_group, across = x_lo * 2 + (1 - core), (1 - x_lo) * 2 + core
    here_weights = weight(group, group), weight(twin_group, group)
    there_weights = weight(group, across), weight(twin_group, across)

    def x_partial(what, chunk):
        p, (own_weight, twin_weight) = {
            OWN: (0, here_weights), NEAR: (0, there_weights), FAR: (1, there_weights), OPPOSITE: (1, here_weights)}[what]
        own, other = tsum[p, part(chunk)], unpacked(sq_in.at[p, chunk])
        return jnp.concatenate(
            [own[:, t * LANES:(t + 1) * LANES] * own_weight + other[:, t * LANES:(t + 1) * LANES] * twin_weight
             for t in range(tiles)], axis=1)

    def x_get(what, chunk):
        arrived(("gx", what, chunk), xq_in.at[what, chunk], near)
        return unpacked(xq_in.at[what, chunk])

    def x_put(what, chunk):
        value = x_partial(what, chunk)
        if what == (FAR if chunk == A else NEAR):
            value = value + x_get(OPPOSITE, chunk)
        packed(xq_out.at[what, chunk], value)
        peer = {NEAR: near, FAR: far, OPPOSITE: near if chunk == A else far}[what]
        send(("gx", what, chunk), xq_out.at[what, chunk], xq_in.at[what, chunk], peer)

    def write(out, chunk, value):
        out[0, part(chunk), :] = value

    x_pass(NEAR, 0)
    x_pass(FAR, 3)
    x_pass(NEAR, 1)
    x_pass(FAR, 4)
    choose(0, 0)
    y_send(1, 1, 0, 0)
    y_send(1, -1, 0, 0)
    x_pass(NEAR, 2)
    x_pass(FAR, 5)
    z_pass(1, 1, A)
    z_pass(1, -1, B)
    choose(0, 1)
    y_send(1, 1, 0, 1)
    y_send(1, -1, 0, 1)
    x_pass(NEAR, 3)
    x_pass(FAR, 0)
    choose(0, 2)
    y_send(1, 1, 0, 2)
    y_send(1, -1, 0, 2)
    x_pass(NEAR, 4)
    x_pass(FAR, 1)
    choose(0, 3)
    y_send(1, -1, 0, 3)
    y_send(1, 1, 0, 3)
    x_pass(NEAR, 5)
    x_pass(FAR, 2)
    z_pass(1, 1, B)
    z_pass(1, -1, A)
    y_pass(1, 1, 0, 0)
    y_pass(1, -1, 0, 0)
    choose(0, 4)
    y_send(1, -1, 0, 4)
    y_send(1, 1, 0, 4)
    x_pass(OPPOSITE, 3)
    x_pass(OPPOSITE, 0)
    y_pass(1, 1, 0, 1)
    y_pass(1, -1, 0, 1)
    choose(0, 5)
    y_send(1, -1, 0, 5)
    y_send(1, 1, 0, 5)
    x_pass(OPPOSITE, 4)
    x_pass(OPPOSITE, 1)
    y_pass(1, 1, 0, 2)
    y_pass(1, -1, 0, 2)
    choose(1, 3)
    y_send(1, -1, 1, 3)
    choose(1, 0)
    y_send(1, 1, 1, 0)
    x_pass(OPPOSITE, 5)
    x_pass(OPPOSITE, 2)
    z_pass(2, 1, A)
    z_pass(2, -1, B)
    y_pass(1, 1, 0, 3)
    y_pass(1, -1, 0, 3)
    choose(1, 4)
    y_send(1, -1, 1, 4)
    choose(1, 1)
    y_send(1, 1, 1, 1)
    y_pass(2, 1, 0, 0)
    y_pass(1, -1, 0, 4)
    choose(1, 5)
    y_send(1, -1, 1, 5)
    choose(1, 2)
    y_send(1, 1, 1, 2)
    y_pass(1, 1, 0, 4)
    y_pass(1, -1, 0, 5)
    y_send(1, 1, 1, 3)
    y_send(1, -1, 1, 0)
    y_send(1, 1, 1, 4)
    y_send(1, -1, 1, 1)
    y_send(1, 1, 1, 5)
    y_send(1, -1, 1, 2)
    z_pass(2, 1, B)
    z_pass(2, -1, A)
    label_columns((0, 1, 7, 2))
    y_pass(2, 1, 0, 1)
    y_pass(1, -1, 1, 3)
    y_pass(1, 1, 0, 5)
    y_pass(2, -1, 0, 3)
    y_pass(2, 1, 0, 2)
    y_pass(1, -1, 1, 4)
    z_pass(3, 1, A)
    z_pass(3, -1, B)
    y_pass(1, 1, 1, 0)
    y_pass(2, -1, 0, 4)
    y_pass(1, 1, 1, 1)
    y_pass(1, -1, 1, 5)
    y_pass(1, 1, 1, 2)
    y_pass(2, -1, 0, 5)
    z_pass(3, 1, B)
    z_pass(3, -1, A)
    label_columns((6, 3, 5))
    slope_tiles(0, 2, 0, 3 * LANES)
    y_pass(1, 1, 1, 3)
    y_pass(1, -1, 1, 0)
    y_pass(1, 1, 1, 4)
    y_pass(1, -1, 1, 1)
    y_pass(1, 1, 1, 5)
    y_pass(1, -1, 1, 2)
    slope_tiles(0, 2, 3 * LANES, 5 * LANES)
    z_pass(4, 1, A)
    z_pass(4, -1, B)
    label_columns((4,))
    slope_tiles(2, 1, 0, 3 * LANES)
    grad_texts(0, 4)
    y_puts[0](1, 1, A)
    y_puts[0](1, -1, B)
    slope_tiles(2, 1, 3 * LANES, 5 * LANES)
    y_pass(2, 1, 1, 0)
    y_pass(2, -1, 1, 3)
    y_pass(2, 1, 1, 1)
    y_pass(2, -1, 1, 4)
    y_pass(2, 1, 1, 2)
    y_pass(2, -1, 1, 5)
    slope_tiles(0, 3, 5 * LANES, 6 * LANES)

    loss_send(0)
    grad_texts(7, 1)
    y_puts[1](1, 1, A)
    y_puts[1](1, -1, B)
    grad_images(5, 3)
    z_put(1, 1, A)
    z_put(1, -1, B)
    z_put(2, 1, B)
    z_put(2, -1, A)
    grad_texts(4, 3)
    y_puts[1](2, 1, B)
    y_puts[1](2, -1, A)
    grad_images(0, 5)
    loss_get(0)
    loss_send(1)
    y_puts[1](2, 1, A)
    y_puts[1](2, -1, B)
    z_put(2, 1, A)
    z_put(2, -1, B)
    y_puts[0](2, 1, A)
    y_puts[0](2, -1, A)
    y_puts[0](2, -1, B)
    y_puts[0](2, 1, B)
    z_put(3, 1, B)
    z_put(3, -1, A)
    loss_get(1)
    loss_send(2)
    z_put(3, 1, A)
    z_put(3, -1, B)
    y_finish(1, A)
    y_finish(1, B)
    loss_get(2)
    loss_send(3)
    z_put(4, 1, B)
    z_put(4, -1, A)
    twin_get(1, A)
    x_put(OPPOSITE, A)
    twin_get(1, B)
    x_put(OPPOSITE, B)
    x_put(FAR, B)
    y_finish(0, A)
    z_put(4, 1, A)
    z_put(4, -1, B)
    twin_get(0, A)
    x_put(NEAR, A)
    y_finish(0, B)
    x_put(FAR, A)
    twin_get(0, B)
    x_put(NEAR, B)
    loss_get(3)
    loss_out[0] = jnp.sum(loss_acc[4]) / total_pairs
    for chunk in (A, B):
        write(img_out, chunk, z_last(chunk))
    for chunk in (A, B):
        write(txt_out, chunk, x_partial(OWN, chunk) + x_get(NEAR, chunk) + x_get(FAR, chunk))
    for copy in pending:
        copy.wait_send()


def shards(image_embeds, text_embeds, positives, partner, log_temp, bias):
    _, rows, width = image_embeds.shape
    half, tiles = rows // 2, width // LANES
    message = (tiles * half + SCALE_ROWS, LANES)
    n_i, n_t = NZ * rows, 2 * NY * rows
    cycle, groups = lax.axis_size("blk"), lax.axis_size("group")
    total_pairs = groups * rows * cycle * cycle
    vmem = pl.BlockSpec(memory_space=pltpu.VMEM)
    smem = pl.BlockSpec(memory_space=pltpu.SMEM)
    hbm = pl.BlockSpec(memory_space=pltpu.HBM)
    in_hbm = functools.partial(pltpu.with_memory_space_constraint, memory_space=pltpu.HBM)
    f32, bf16, i16, i32 = jnp.float32, jnp.bfloat16, jnp.int16, jnp.int32
    copies = 176
    images, texts, loss = pl.pallas_call(
        functools.partial(kernel, float(total_pairs)),
        out_shape=(jax.ShapeDtypeStruct((1, rows, width), f32), jax.ShapeDtypeStruct((1, rows, width), f32),
                   jax.ShapeDtypeStruct((1,), f32)),
        in_specs=[hbm] * 6,
        out_specs=(vmem, vmem, smem),
        scratch_shapes=[
            pltpu.SMEM(partner.shape, i32),
            pltpu.SMEM((1,), f32),
            pltpu.SMEM((1,), f32),
            pltpu.VMEM((1, rows), i32),
            pltpu.VMEM((n_i, width), bf16),
            pltpu.VMEM((n_t, width), bf16),
            pltpu.VMEM((2, NX, rows, width), bf16),
            pltpu.VMEM((NZ, 8, LANES), i32),
            pltpu.VMEM((n_i, LANES), i32),
            pltpu.VMEM((n_i, n_t), bf16),
            pltpu.VMEM((n_t, n_i), bf16),
            pltpu.VMEM((n_i, width), f32),
            pltpu.VMEM((n_t, width), f32),
            pltpu.VMEM((2, rows, width), f32),
            pltpu.VMEM((5, 8, LANES), f32),
            pltpu.VMEM((4, NZ, 8, LANES), f32),
            pltpu.VMEM((2, NZ, *message), i16),
            pltpu.VMEM((2, NZ, *message), i16),
            pltpu.VMEM((2, 2, NY, *message), i16),
            pltpu.VMEM((2, 2, NY, *message), i16),
            pltpu.VMEM((2, 2, *message), i16),
            pltpu.VMEM((2, 2, *message), i16),
            pltpu.VMEM((NX, 2, *message), i16),
            pltpu.VMEM((NX, 2, *message), i16),
            pltpu.SemaphoreType.DMA((copies,)),
            pltpu.SemaphoreType.DMA((copies,)),
            pltpu.SemaphoreType.DMA((6,)),
        ],
        compiler_params=pltpu.CompilerParams(
            collective_id=0, has_side_effects=True, vmem_limit_bytes=48 * 1024 * 1024),
    )(in_hbm(partner), log_temp, bias, in_hbm(image_embeds), in_hbm(text_embeds), in_hbm(positives))
    temper = jnp.exp(log_temp[0])
    return temper * images, temper * texts, loss


def solution(mesh):
    in_specs = (P("group", "blk", None), P("group", "blk", None), P("group", "blk"), P(), P(), P())
    out_specs = (P("group", "blk", None), P("group", "blk", None), P())
    return jax.shard_map(shards, mesh=mesh, in_specs=in_specs, out_specs=out_specs, check_vma=False)
```

```python
import functools

import jax
import jax.numpy as jnp
from jax import lax
from jax.experimental import pallas as pl
from jax.experimental.pallas import tpu as pltpu
from jax.sharding import PartitionSpec as P

NZ, NX, NY = 8, 4, 4
LANES = 128
PIECES = 6
SCALE_ROWS = 16
TOP = 14.9657842846620869


def kernel(total_pairs, partner_in, temp_in, bias_in, img_in, txt_in, lab_in,
           img_out, txt_out, loss_out,
           partner_ref, temp_ref, bias_ref, lab_own, ibuf, tbuf, xbuf, labrow, labcol, slopes, slopes_t, gi, gt, tsum,
           loss_acc, loss_in, zq_out, zq_in, yq_out, yq_in, sq_out, sq_in, xq_out, xq_in,
           send_sems, recv_sems, local_sems):
    rows, width = img_in.shape[1], img_in.shape[2]
    half, piece = rows // 2, rows // PIECES
    tiles = width // LANES
    A, B = 0, 1
    OWN, NEAR, FAR, OPPOSITE = 0, 1, 2, 3

    local = [pltpu.make_async_copy(src, dst, local_sems.at[k]) for k, (src, dst) in enumerate((
        (txt_in.at[0], xbuf.at[0, OWN]), (img_in.at[0], ibuf.at[0:rows]), (lab_in, lab_own),
        (partner_in, partner_ref), (temp_in, temp_ref), (bias_in, bias_ref)))]
    for copy in local:
        copy.start()

    blk, group = lax.axis_index("blk"), lax.axis_index("group")
    z, x_hi, y = blk // (NX // 2 * NY), (blk // NY) % (NX // 2), blk % NY
    x_lo, core = group // 2, group % 2
    x = x_hi * 2 + x_lo

    def device(z_at, x_at, y_at, core_at):
        return ((z_at % NZ) * (NX // 2 * NY) + ((x_at % NX) // 2) * NY + y_at % NY, (x_at % 2) * 2 + core_at)

    z_up, z_down = device(z + 1, x, y, core), device(z + NZ - 1, x, y, core)
    y_up, y_down = device(z, x, y + 1, core), device(z, x, y + NY - 1, core)
    near, far = device(z, x + 1 + 2 * x_lo, y, core), device(z, x + 3 - 2 * x_lo, y, core)
    twin = device(z, x, y, 1 - core)
    x_others = [(d, device(z, x + d, y, core)) for d in range(1, NX)]
    y_others = [(d, device(z, x, y + d, core)) for d in range(1, NY)]
    z_others = [(d, device(z + d, x, y, core)) for d in range(1, NZ)]

    greeted = [twin] + [peer for _, peer in x_others + y_others + z_others]
    barrier = pltpu.get_barrier_semaphore()
    for peer in greeted:
        pl.semaphore_signal(barrier, inc=1, device_id=peer, device_id_type=pl.DeviceIdType.MESH)
    pl.semaphore_wait(barrier, len(greeted))

    places, pending = {}, []

    def copy_of(name, src, dst, peer):
        place = places.setdefault(name, len(places))
        return pltpu.make_async_remote_copy(
            src_ref=src, dst_ref=dst, send_sem=send_sems.at[place], recv_sem=recv_sems.at[place],
            device_id=peer, device_id_type=pl.DeviceIdType.MESH)

    def send(name, src, dst, peer):
        copy = copy_of(name, src, dst, peer)
        copy.start()
        pending.append(copy)

    def arrived(name, dst, peer):
        copy_of(name, dst, dst, peer).wait_recv()

    def part(chunk):
        return pl.ds(chunk * half, half)

    order, text_order = (0, 1, 7, 2, 6, 3, 5, 4), (0, 1, 3, 2)

    def image_at(rel, chunk=0):
        return order.index(rel % NZ) * rows + chunk * half

    def text_at(rel, p, chunk=0):
        return (p * NY + text_order.index(rel % NY)) * rows + chunk * half

    def image_slot(rel, chunk):
        return ibuf.at[pl.ds(image_at(rel, chunk), half)]

    def text_slot(rel, p, k):
        return tbuf.at[pl.ds(text_at(rel, p) + k * piece, piece)]

    def x_slot(side, which, k):
        return xbuf.at[side, which, pl.ds(k * piece, piece)]

    def low(k):
        return k < PIECES // 2

    def z_send(hop, way, chunk):
        source = img_in.at[0, part(chunk)] if hop == 1 else image_slot(-way * (hop - 1), chunk)
        send(("z", hop, way, chunk), source, image_slot(-way * hop, chunk), z_up if way > 0 else z_down)

    def label_send(hop, way):
        send(("label", hop, way), labrow.at[(-way * (hop - 1)) % NZ], labrow.at[(-way * hop) % NZ],
             z_up if way > 0 else z_down)

    def z_pass(hop, way, chunk):
        first = chunk == (A if way > 0 else B)
        arrived(("z", hop, way, chunk), image_slot(-way * hop, chunk), z_up)
        if hop < NZ // 2 - 1 or (hop == NZ // 2 - 1 and first):
            z_send(hop + 1, way, chunk)
        if not first or (hop == NZ // 2 and way > 0):
            arrived(("label", hop, way), labrow.at[(-way * hop) % NZ], z_up)
            if hop < NZ // 2 - 1 or (hop == NZ // 2 - 1 and way > 0):
                label_send(hop + 1, way)

    def x_send(what, k):
        src, peer = {NEAR: (OWN, near), FAR: (OWN, far), OPPOSITE: (NEAR, far) if low(k) else (FAR, near)}[what]
        source = txt_in.at[0, pl.ds(k * piece, piece)] if src == OWN else x_slot(0, src, k)
        send(("x", what, k), source, x_slot(0, what, k), peer)

    def twin_send(what, k):
        source = txt_in.at[0, pl.ds(k * piece, piece)] if what == OWN else x_slot(0, what, k)
        send(("twin", what, k), source, x_slot(1, what, k), twin)

    def x_pass(what, k):
        arrived(("x", what, k), x_slot(0, what, k), near)
        if what == (NEAR if low(k) else FAR):
            x_send(OPPOSITE, k)
        twin_send(what, k)

    def y_send(hop, way, p, k):
        send(("y", hop, way, p, k), text_slot(-way * (hop - 1), p, k), text_slot(-way * hop, p, k),
             y_up if way > 0 else y_down)

    def y_pass(hop, way, p, k):
        arrived(("y", hop, way, p, k), text_slot(-way * hop, p, k), y_up)
        if hop == 1 and low(k) == (way > 0):
            y_send(2, way, p, k)

    def choose(p, k):
        target = partner_ref[group]
        same_side, same_core = target // 2 == x_lo, target % 2 == core
        here, there = (OWN, NEAR) if p == 0 else (OPPOSITE, FAR)
        for what in (here, there):
            arrived(("twin", what, k), x_slot(1, what, k), twin)
        here, there = (jnp.where(same_core, xbuf[0, what, pl.ds(k * piece, piece)], xbuf[1, what, pl.ds(k * piece, piece)])
                       for what in (here, there))
        tbuf[pl.ds(text_at(0, p) + k * piece, piece), :] = jnp.where(same_side, here, there)

    x_send(NEAR, 0)
    x_send(FAR, 3)
    twin_send(OWN, 0)
    z_send(1, 1, A)
    z_send(1, -1, B)
    z_send(1, 1, B)
    z_send(1, -1, A)
    x_send(NEAR, 1)
    x_send(FAR, 4)
    twin_send(OWN, 1)
    x_send(NEAR, 2)
    x_send(FAR, 5)
    twin_send(OWN, 2)
    x_send(NEAR, 3)
    x_send(FAR, 0)
    twin_send(OWN, 3)
    x_send(NEAR, 4)
    x_send(FAR, 1)
    twin_send(OWN, 4)
    x_send(NEAR, 5)
    x_send(FAR, 2)
    twin_send(OWN, 5)
    local[2].wait()
    labrow[0] = jnp.zeros((8, LANES), jnp.int32)
    labrow[0, 0:1, 0:rows] = lab_own[...]
    label_send(1, 1)
    label_send(1, -1)
    for copy in local[:2] + local[3:]:
        copy.wait()

    temper = jnp.exp(jnp.full((1, LANES), temp_ref[0], jnp.float32))
    offset = jnp.full((1, LANES), bias_ref[0], jnp.float32)
    loss_acc[0] = jnp.zeros((8, LANES), jnp.float32)
    n_i, n_t = NZ * rows, 2 * NY * rows

    def label_columns(rels):
        for rel in rels:
            column = jnp.broadcast_to(labrow[rel, 0:1, :], (LANES, LANES)).T
            labcol[image_at(rel):image_at(rel) + rows, :] = column[:rows]

    def slope_tiles(first, count, left, right):
        wide = 2 * LANES
        blocks = [(p, rel) for p in (0, 1) for rel in text_order]

        def text_rows(at):
            column = lax.broadcasted_iota(jnp.int32, (1, LANES), 1) + at
            found = column
            for b, (p, rel) in enumerate(blocks):
                owner = (z * (NX // 2) + (x_hi + p) % 2) * NY + (y + rel) % NY
                found = jnp.where(column >= b * rows, column + (owner - b) * rows, found)
            return found

        def step(k, carry):
            top = pl.multiple_of(k * wide, wide)
            for start in range(left, right, wide):
                stop = min(start + wide, right)
                dots = lax.dot_general(ibuf[pl.ds(top, wide), :], tbuf[start:stop, :], (((1,), (1,)), ((), ())),
                                       preferred_element_type=jnp.float32)
                for at in range(start, stop, LANES):
                    logits = temper * dots[:, at - start:at - start + LANES] + offset
                    hit = labcol[pl.ds(top, wide), :] == text_rows(at)
                    margin = jnp.where(hit, -logits, logits)
                    small = jnp.exp(-jnp.abs(logits))
                    base = 1.0 + small
                    inverse = 1.0 / base
                    log_part = jnp.log(base) + (small - (base - 1.0)) * inverse
                    loss = jnp.maximum(margin, 0.0) + log_part
                    loss_acc[0] += jnp.sum(loss.reshape(wide // 8, 8, LANES), axis=0)
                    slope = jnp.where(margin >= 0.0, 1.0, small) * inverse
                    slope = jnp.where(hit, -slope, slope).astype(jnp.bfloat16)
                    slopes[pl.ds(top, wide), at:at + LANES] = slope
                    slopes_t[at:at + LANES, pl.ds(top, wide)] = slope.T
            return carry

        lax.fori_loop(first, first + count, step, 0)

    def grad_images(first, count):
        gi[first * rows:(first + count) * rows, :] = jnp.dot(
            slopes[first * rows:(first + count) * rows, :], tbuf[...], preferred_element_type=jnp.float32)

    def grad_texts(first, count):
        gt[first * rows:(first + count) * rows, :] = jnp.dot(
            slopes_t[first * rows:(first + count) * rows, :], ibuf[...], preferred_element_type=jnp.float32)

    def packed(out, value):
        tops = jnp.max(jnp.abs(value).reshape(half // SCALE_ROWS, SCALE_ROWS, width), axis=0)
        top = tops[:, 0:LANES]
        for t in range(1, tiles):
            top = jnp.maximum(top, tops[:, t * LANES:(t + 1) * LANES])
        exponent = jnp.ceil(jnp.log2(jnp.maximum(top, 1e-30)))
        inverse = jnp.concatenate([jnp.exp2(TOP - exponent)] * (half // SCALE_ROWS), axis=0)
        out[tiles * half:tiles * half + SCALE_ROWS, :] = exponent.astype(jnp.int16)
        for t in range(tiles):
            scaled = jnp.round(value[:, t * LANES:(t + 1) * LANES] * inverse)
            out[t * half:(t + 1) * half, :] = scaled.astype(jnp.int32).astype(jnp.int16)

    def unpacked(message):
        exponent = message[tiles * half:tiles * half + SCALE_ROWS, :].astype(jnp.int32).astype(jnp.float32)
        scale = jnp.concatenate([jnp.exp2(exponent - TOP)] * (half // SCALE_ROWS), axis=0)
        return jnp.concatenate(
            [message[t * half:(t + 1) * half, :].astype(jnp.int32).astype(jnp.float32) * scale for t in range(tiles)],
            axis=1)

    def ring(kind, n, out, inbox, up, down, partial):
        halfway = n // 2

        def slot(hop, way, chunk):
            return (0 if way > 0 else 1), 2 * (hop - 1) + chunk

        def get(hop, way, chunk):
            box = inbox.at[slot(hop, way, chunk)]
            arrived((kind, hop, way, chunk), box, up)
            return unpacked(box)

        def put(hop, way, chunk):
            value = partial(way * (halfway + 1 - hop), chunk)
            fresh = hop == 1 or (hop == 2 and chunk == (B if way > 0 else A))
            if not fresh:
                value = value + get(hop - 1, way, chunk)
            at = slot(hop, way, chunk)
            packed(out.at[at], value)
            send((kind, hop, way, chunk), out.at[at], inbox.at[at], up if way > 0 else down)

        def last(chunk):
            return partial(0, chunk) + get(halfway, 1, chunk) + get(halfway, -1, chunk)

        return put, last

    z_put, z_last = ring("gz", NZ, zq_out, zq_in, z_up, z_down,
                         lambda rel, chunk: gi[image_at(rel, chunk):image_at(rel, chunk) + half, :])
    y_puts, y_lasts = [], []
    for p in (0, 1):
        put, last = ring(("gy", p), NY, yq_out.at[p], yq_in.at[p], y_up, y_down,
                         lambda rel, chunk, p=p: gt[text_at(rel, p, chunk):text_at(rel, p, chunk) + half, :])
        y_puts.append(put)
        y_lasts.append(last)

    loss_stages = [(z, z_others), (x, x_others), (core, [(1, twin)]), (y, y_others)]

    def loss_send(stage):
        at, others = loss_stages[stage]
        loss_in[stage, at] = loss_acc[stage]
        for d, peer in others:
            send(("loss", stage, d), loss_acc.at[stage], loss_in.at[stage, at], peer)

    def loss_get(stage):
        at, others = loss_stages[stage]
        for d, peer in others:
            arrived(("loss", stage, d), loss_in.at[stage, at], peer)
        total = loss_in[stage, 0]
        for k in range(1, len(others) + 1):
            total = total + loss_in[stage, k]
        loss_acc[stage + 1] = total

    def y_finish(p, chunk):
        tsum[p, part(chunk)] = y_lasts[p](chunk)
        packed(sq_out.at[p, chunk], tsum[p, part(chunk)])
        send(("gs", p, chunk), sq_out.at[p, chunk], sq_in.at[p, chunk], twin)

    def twin_get(p, chunk):
        arrived(("gs", p, chunk), sq_in.at[p, chunk], twin)

    def weight(who, home):
        return jnp.full((1, LANES), jnp.where(partner_ref[who] == home, 1.0, 0.0), jnp.float32)

    twin_group, across = x_lo * 2 + (1 - core), (1 - x_lo) * 2 + core
    here_weights = weight(group, group), weight(twin_group, group)
    there_weights = weight(group, across), weight(twin_group, across)

    def x_partial(what, chunk):
        p, (own_weight, twin_weight) = {
            OWN: (0, here_weights), NEAR: (0, there_weights), FAR: (1, there_weights), OPPOSITE: (1, here_weights)}[what]
        own, other = tsum[p, part(chunk)], unpacked(sq_in.at[p, chunk])
        return jnp.concatenate(
            [own[:, t * LANES:(t + 1) * LANES] * own_weight + other[:, t * LANES:(t + 1) * LANES] * twin_weight
             for t in range(tiles)], axis=1)

    def x_get(what, chunk):
        arrived(("gx", what, chunk), xq_in.at[what, chunk], near)
        return unpacked(xq_in.at[what, chunk])

    def x_put(what, chunk):
        value = x_partial(what, chunk)
        if what == (FAR if chunk == A else NEAR):
            value = value + x_get(OPPOSITE, chunk)
        packed(xq_out.at[what, chunk], value)
        peer = {NEAR: near, FAR: far, OPPOSITE: near if chunk == A else far}[what]
        send(("gx", what, chunk), xq_out.at[what, chunk], xq_in.at[what, chunk], peer)

    def write(out, chunk, value):
        out[0, part(chunk), :] = value

    x_pass(NEAR, 0)
    x_pass(FAR, 3)
    x_pass(NEAR, 1)
    x_pass(FAR, 4)
    choose(0, 0)
    y_send(1, 1, 0, 0)
    y_send(1, -1, 0, 0)
    x_pass(NEAR, 2)
    x_pass(FAR, 5)
    z_pass(1, 1, A)
    z_pass(1, -1, B)
    choose(0, 1)
    y_send(1, 1, 0, 1)
    y_send(1, -1, 0, 1)
    x_pass(NEAR, 3)
    x_pass(FAR, 0)
    choose(0, 2)
    y_send(1, 1, 0, 2)
    y_send(1, -1, 0, 2)
    x_pass(NEAR, 4)
    x_pass(FAR, 1)
    choose(0, 3)
    y_send(1, -1, 0, 3)
    y_send(1, 1, 0, 3)
    x_pass(NEAR, 5)
    x_pass(FAR, 2)
    z_pass(1, 1, B)
    z_pass(1, -1, A)
    y_pass(1, 1, 0, 0)
    y_pass(1, -1, 0, 0)
    choose(0, 4)
    y_send(1, -1, 0, 4)
    y_send(1, 1, 0, 4)
    x_pass(OPPOSITE, 3)
    x_pass(OPPOSITE, 0)
    y_pass(1, 1, 0, 1)
    y_pass(1, -1, 0, 1)
    choose(0, 5)
    y_send(1, -1, 0, 5)
    y_send(1, 1, 0, 5)
    x_pass(OPPOSITE, 4)
    x_pass(OPPOSITE, 1)
    y_pass(1, 1, 0, 2)
    y_pass(1, -1, 0, 2)
    choose(1, 3)
    y_send(1, -1, 1, 3)
    choose(1, 0)
    y_send(1, 1, 1, 0)
    x_pass(OPPOSITE, 5)
    x_pass(OPPOSITE, 2)
    z_pass(2, 1, A)
    z_pass(2, -1, B)
    y_pass(1, 1, 0, 3)
    y_pass(1, -1, 0, 3)
    choose(1, 4)
    y_send(1, -1, 1, 4)
    choose(1, 1)
    y_send(1, 1, 1, 1)
    y_pass(2, 1, 0, 0)
    y_pass(1, -1, 0, 4)
    choose(1, 5)
    y_send(1, -1, 1, 5)
    choose(1, 2)
    y_send(1, 1, 1, 2)
    y_pass(1, 1, 0, 4)
    y_pass(1, -1, 0, 5)
    y_send(1, 1, 1, 3)
    y_send(1, -1, 1, 0)
    y_send(1, 1, 1, 4)
    y_send(1, -1, 1, 1)
    y_send(1, 1, 1, 5)
    y_send(1, -1, 1, 2)
    z_pass(2, 1, B)
    z_pass(2, -1, A)
    label_columns((0, 1, 7, 2))
    y_pass(2, 1, 0, 1)
    y_pass(1, -1, 1, 3)
    y_pass(1, 1, 0, 5)
    y_pass(2, -1, 0, 3)
    y_pass(2, 1, 0, 2)
    y_pass(1, -1, 1, 4)
    z_pass(3, 1, A)
    z_pass(3, -1, B)
    y_pass(1, 1, 1, 0)
    y_pass(2, -1, 0, 4)
    y_pass(1, 1, 1, 1)
    y_pass(1, -1, 1, 5)
    y_pass(1, 1, 1, 2)
    y_pass(2, -1, 0, 5)
    z_pass(3, 1, B)
    z_pass(3, -1, A)
    label_columns((6, 3, 5))
    slope_tiles(0, 2, 0, 3 * LANES)
    y_pass(1, 1, 1, 3)
    y_pass(1, -1, 1, 0)
    y_pass(1, 1, 1, 4)
    y_pass(1, -1, 1, 1)
    y_pass(1, 1, 1, 5)
    y_pass(1, -1, 1, 2)
    slope_tiles(0, 2, 3 * LANES, 5 * LANES)
    z_pass(4, 1, A)
    z_pass(4, -1, B)
    label_columns((4,))
    slope_tiles(2, 1, 0, 3 * LANES)
    grad_texts(0, 4)
    y_puts[0](1, 1, A)
    y_puts[0](1, -1, B)
    slope_tiles(2, 1, 3 * LANES, 5 * LANES)
    y_pass(2, 1, 1, 0)
    y_pass(2, -1, 1, 3)
    y_pass(2, 1, 1, 1)
    y_pass(2, -1, 1, 4)
    y_pass(2, 1, 1, 2)
    y_pass(2, -1, 1, 5)
    slope_tiles(0, 3, 5 * LANES, 6 * LANES)

    loss_send(0)
    grad_texts(7, 1)
    y_puts[1](1, 1, A)
    y_puts[1](1, -1, B)
    grad_images(5, 3)
    z_put(1, 1, A)
    z_put(1, -1, B)
    z_put(2, 1, B)
    z_put(2, -1, A)
    grad_texts(4, 3)
    y_puts[1](2, 1, B)
    y_puts[1](2, -1, A)
    grad_images(0, 5)
    loss_get(0)
    loss_send(1)
    y_puts[1](2, 1, A)
    y_puts[1](2, -1, B)
    z_put(2, 1, A)
    z_put(2, -1, B)
    y_puts[0](2, 1, A)
    y_puts[0](2, -1, A)
    y_puts[0](2, -1, B)
    y_puts[0](2, 1, B)
    z_put(3, 1, B)
    z_put(3, -1, A)
    loss_get(1)
    loss_send(2)
    z_put(3, 1, A)
    z_put(3, -1, B)
    y_finish(1, A)
    y_finish(1, B)
    loss_get(2)
    loss_send(3)
    z_put(4, 1, B)
    z_put(4, -1, A)
    twin_get(1, A)
    x_put(OPPOSITE, A)
    twin_get(1, B)
    x_put(OPPOSITE, B)
    x_put(FAR, B)
    y_finish(0, A)
    z_put(4, 1, A)
    z_put(4, -1, B)
    twin_get(0, A)
    x_put(NEAR, A)
    y_finish(0, B)
    x_put(FAR, A)
    twin_get(0, B)
    x_put(NEAR, B)
    loss_get(3)
    loss_out[0] = jnp.sum(loss_acc[4]) / total_pairs
    for chunk in (A, B):
        write(img_out, chunk, z_last(chunk))
    for chunk in (A, B):
        write(txt_out, chunk, x_partial(OWN, chunk) + x_get(NEAR, chunk) + x_get(FAR, chunk))
    for copy in pending:
        copy.wait_send()


def shards(image_embeds, text_embeds, positives, partner, log_temp, bias):
    _, rows, width = image_embeds.shape
    half, tiles = rows // 2, width // LANES
    message = (tiles * half + SCALE_ROWS, LANES)
    n_i, n_t = NZ * rows, 2 * NY * rows
    cycle, groups = lax.axis_size("blk"), lax.axis_size("group")
    total_pairs = groups * rows * cycle * cycle
    vmem = pl.BlockSpec(memory_space=pltpu.VMEM)
    smem = pl.BlockSpec(memory_space=pltpu.SMEM)
    hbm = pl.BlockSpec(memory_space=pltpu.HBM)
    in_hbm = functools.partial(pltpu.with_memory_space_constraint, memory_space=pltpu.HBM)
    f32, bf16, i16, i32 = jnp.float32, jnp.bfloat16, jnp.int16, jnp.int32
    copies = 176
    images, texts, loss = pl.pallas_call(
        functools.partial(kernel, float(total_pairs)),
        out_shape=(jax.ShapeDtypeStruct((1, rows, width), f32), jax.ShapeDtypeStruct((1, rows, width), f32),
                   jax.ShapeDtypeStruct((1,), f32)),
        in_specs=[hbm] * 6,
        out_specs=(vmem, vmem, smem),
        scratch_shapes=[
            pltpu.SMEM(partner.shape, i32),
            pltpu.SMEM((1,), f32),
            pltpu.SMEM((1,), f32),
            pltpu.VMEM((1, rows), i32),
            pltpu.VMEM((n_i, width), bf16),
            pltpu.VMEM((n_t, width), bf16),
            pltpu.VMEM((2, NX, rows, width), bf16),
            pltpu.VMEM((NZ, 8, LANES), i32),
            pltpu.VMEM((n_i, LANES), i32),
            pltpu.VMEM((n_i, n_t), bf16),
            pltpu.VMEM((n_t, n_i), bf16),
            pltpu.VMEM((n_i, width), f32),
            pltpu.VMEM((n_t, width), f32),
            pltpu.VMEM((2, rows, width), f32),
            pltpu.VMEM((5, 8, LANES), f32),
            pltpu.VMEM((4, NZ, 8, LANES), f32),
            pltpu.VMEM((2, NZ, *message), i16),
            pltpu.VMEM((2, NZ, *message), i16),
            pltpu.VMEM((2, 2, NY, *message), i16),
            pltpu.VMEM((2, 2, NY, *message), i16),
            pltpu.VMEM((2, 2, *message), i16),
            pltpu.VMEM((2, 2, *message), i16),
            pltpu.VMEM((NX, 2, *message), i16),
            pltpu.VMEM((NX, 2, *message), i16),
            pltpu.SemaphoreType.DMA((copies,)),
            pltpu.SemaphoreType.DMA((copies,)),
            pltpu.SemaphoreType.DMA((6,)),
        ],
        compiler_params=pltpu.CompilerParams(
            collective_id=0, has_side_effects=True, vmem_limit_bytes=48 * 1024 * 1024),
    )(in_hbm(partner), log_temp, bias, in_hbm(image_embeds), in_hbm(text_embeds), in_hbm(positives))
    temper = jnp.exp(log_temp[0])
    return temper * images, temper * texts, loss


def solution(mesh):
    in_specs = (P("group", "blk", None), P("group", "blk", None), P("group", "blk"), P(), P(), P())
    out_specs = (P("group", "blk", None), P("group", "blk", None), P())
    return jax.shard_map(shards, mesh=mesh, in_specs=in_specs, out_specs=out_specs, check_vma=False)
```

```python
import functools

import jax
import jax.numpy as jnp
from jax import lax
from jax.experimental import pallas as pl
from jax.experimental.pallas import tpu as pltpu
from jax.sharding import PartitionSpec as P

NZ, NX, NY = 8, 4, 4
LANES = 128
PIECES = 6
SCALE_ROWS = 16
TOP = 14.9657842846620869


def kernel(total_pairs, partner_in, temp_in, bias_in, img_in, txt_in, lab_in,
           img_out, txt_out, loss_out,
           partner_ref, temp_ref, bias_ref, lab_own, ibuf, tbuf, xbuf, labrow, labcol, slopes, slopes_t, gi, gt, tsum,
           loss_acc, loss_in, zq_out, zq_in, yq_out, yq_in, sq_out, sq_in, xq_out, xq_in,
           send_sems, recv_sems, local_sems):
    rows, width = img_in.shape[1], img_in.shape[2]
    half, piece = rows // 2, rows // PIECES
    tiles = width // LANES
    A, B = 0, 1
    OWN, NEAR, FAR, OPPOSITE = 0, 1, 2, 3

    local = [pltpu.make_async_copy(src, dst, local_sems.at[k]) for k, (src, dst) in enumerate((
        (txt_in.at[0], xbuf.at[0, OWN]), (img_in.at[0], ibuf.at[0:rows]), (lab_in, lab_own),
        (partner_in, partner_ref), (temp_in, temp_ref), (bias_in, bias_ref)))]
    for copy in local:
        copy.start()

    blk, group = lax.axis_index("blk"), lax.axis_index("group")
    z, x_hi, y = blk // (NX // 2 * NY), (blk // NY) % (NX // 2), blk % NY
    x_lo, core = group // 2, group % 2
    x = x_hi * 2 + x_lo

    def device(z_at, x_at, y_at, core_at):
        return ((z_at % NZ) * (NX // 2 * NY) + ((x_at % NX) // 2) * NY + y_at % NY, (x_at % 2) * 2 + core_at)

    z_up, z_down = device(z + 1, x, y, core), device(z + NZ - 1, x, y, core)
    y_up, y_down = device(z, x, y + 1, core), device(z, x, y + NY - 1, core)
    near, far = device(z, x + 1 + 2 * x_lo, y, core), device(z, x + 3 - 2 * x_lo, y, core)
    twin = device(z, x, y, 1 - core)
    x_others = [(d, device(z, x + d, y, core)) for d in range(1, NX)]
    y_others = [(d, device(z, x, y + d, core)) for d in range(1, NY)]
    z_others = [(d, device(z + d, x, y, core)) for d in range(1, NZ)]

    greeted = [twin] + [peer for _, peer in x_others + y_others + z_others]
    barrier = pltpu.get_barrier_semaphore()
    for peer in greeted:
        pl.semaphore_signal(barrier, inc=1, device_id=peer, device_id_type=pl.DeviceIdType.MESH)
    pl.semaphore_wait(barrier, len(greeted))

    places, pending = {}, []

    def copy_of(name, src, dst, peer):
        place = places.setdefault(name, len(places))
        return pltpu.make_async_remote_copy(
            src_ref=src, dst_ref=dst, send_sem=send_sems.at[place], recv_sem=recv_sems.at[place],
            device_id=peer, device_id_type=pl.DeviceIdType.MESH)

    def send(name, src, dst, peer):
        copy = copy_of(name, src, dst, peer)
        copy.start()
        pending.append(copy)

    def arrived(name, dst, peer):
        copy_of(name, dst, dst, peer).wait_recv()

    def part(chunk):
        return pl.ds(chunk * half, half)

    order, text_order = (0, 1, 7, 2, 6, 3, 5, 4), (0, 1, 3, 2)

    def image_at(rel, chunk=0):
        return order.index(rel % NZ) * rows + chunk * half

    def text_at(rel, p, chunk=0):
        return (p * NY + text_order.index(rel % NY)) * rows + chunk * half

    def image_slot(rel, chunk):
        return ibuf.at[pl.ds(image_at(rel, chunk), half)]

    def text_slot(rel, p, k):
        return tbuf.at[pl.ds(text_at(rel, p) + k * piece, piece)]

    def x_slot(side, which, k):
        return xbuf.at[side, which, pl.ds(k * piece, piece)]

    def low(k):
        return k < PIECES // 2

    def z_send(hop, way, chunk):
        source = img_in.at[0, part(chunk)] if hop == 1 else image_slot(-way * (hop - 1), chunk)
        send(("z", hop, way, chunk), source, image_slot(-way * hop, chunk), z_up if way > 0 else z_down)

    def label_send(hop, way):
        send(("label", hop, way), labrow.at[(-way * (hop - 1)) % NZ], labrow.at[(-way * hop) % NZ],
             z_up if way > 0 else z_down)

    def z_pass(hop, way, chunk):
        first = chunk == (A if way > 0 else B)
        arrived(("z", hop, way, chunk), image_slot(-way * hop, chunk), z_up)
        if hop < NZ // 2 - 1 or (hop == NZ // 2 - 1 and first):
            z_send(hop + 1, way, chunk)
        if not first or (hop == NZ // 2 and way > 0):
            arrived(("label", hop, way), labrow.at[(-way * hop) % NZ], z_up)
            if hop < NZ // 2 - 1 or (hop == NZ // 2 - 1 and way > 0):
                label_send(hop + 1, way)

    def x_send(what, k):
        src, peer = {NEAR: (OWN, near), FAR: (OWN, far), OPPOSITE: (NEAR, far) if low(k) else (FAR, near)}[what]
        source = txt_in.at[0, pl.ds(k * piece, piece)] if src == OWN else x_slot(0, src, k)
        send(("x", what, k), source, x_slot(0, what, k), peer)

    def twin_send(what, k):
        source = txt_in.at[0, pl.ds(k * piece, piece)] if what == OWN else x_slot(0, what, k)
        send(("twin", what, k), source, x_slot(1, what, k), twin)

    def x_pass(what, k):
        arrived(("x", what, k), x_slot(0, what, k), near)
        if what == (NEAR if low(k) else FAR):
            x_send(OPPOSITE, k)
        twin_send(what, k)

    def y_send(hop, way, p, k):
        send(("y", hop, way, p, k), text_slot(-way * (hop - 1), p, k), text_slot(-way * hop, p, k),
             y_up if way > 0 else y_down)

    def y_pass(hop, way, p, k):
        arrived(("y", hop, way, p, k), text_slot(-way * hop, p, k), y_up)
        if hop == 1 and low(k) == (way > 0):
            y_send(2, way, p, k)

    def choose(p, k):
        target = partner_ref[group]
        same_side, same_core = target // 2 == x_lo, target % 2 == core
        here, there = (OWN, NEAR) if p == 0 else (OPPOSITE, FAR)
        for what in (here, there):
            arrived(("twin", what, k), x_slot(1, what, k), twin)
        here, there = (jnp.where(same_core, xbuf[0, what, pl.ds(k * piece, piece)], xbuf[1, what, pl.ds(k * piece, piece)])
                       for what in (here, there))
        tbuf[pl.ds(text_at(0, p) + k * piece, piece), :] = jnp.where(same_side, here, there)

    x_send(NEAR, 0)
    x_send(FAR, 3)
    twin_send(OWN, 0)
    z_send(1, 1, A)
    z_send(1, -1, B)
    z_send(1, 1, B)
    z_send(1, -1, A)
    x_send(NEAR, 1)
    x_send(FAR, 4)
    twin_send(OWN, 1)
    x_send(NEAR, 2)
    x_send(FAR, 5)
    twin_send(OWN, 2)
    x_send(NEAR, 3)
    x_send(FAR, 0)
    twin_send(OWN, 3)
    x_send(NEAR, 4)
    x_send(FAR, 1)
    twin_send(OWN, 4)
    x_send(NEAR, 5)
    x_send(FAR, 2)
    twin_send(OWN, 5)
    local[2].wait()
    labrow[0] = jnp.zeros((8, LANES), jnp.int32)
    labrow[0, 0:1, 0:rows] = lab_own[...]
    label_send(1, 1)
    label_send(1, -1)
    for copy in local[:2] + local[3:]:
        copy.wait()

    temper = jnp.exp(jnp.full((1, LANES), temp_ref[0], jnp.float32))
    offset = jnp.full((1, LANES), bias_ref[0], jnp.float32)
    loss_acc[0] = jnp.zeros((8, LANES), jnp.float32)
    n_i, n_t = NZ * rows, 2 * NY * rows

    def label_columns(rels):
        for rel in rels:
            column = jnp.broadcast_to(labrow[rel, 0:1, :], (LANES, LANES)).T
            labcol[image_at(rel):image_at(rel) + rows, :] = column[:rows]

    def slope_tiles(first, count, left, right):
        wide = 2 * LANES
        blocks = [(p, rel) for p in (0, 1) for rel in text_order]

        def text_rows(at):
            column = lax.broadcasted_iota(jnp.int32, (1, LANES), 1) + at
            found = column
            for b, (p, rel) in enumerate(blocks):
                owner = (z * (NX // 2) + (x_hi + p) % 2) * NY + (y + rel) % NY
                found = jnp.where(column >= b * rows, column + (owner - b) * rows, found)
            return found

        def step(k, carry):
            top = pl.multiple_of(k * wide, wide)
            for start in range(left, right, wide):
                stop = min(start + wide, right)
                dots = lax.dot_general(ibuf[pl.ds(top, wide), :], tbuf[start:stop, :], (((1,), (1,)), ((), ())),
                                       preferred_element_type=jnp.float32)
                for at in range(start, stop, LANES):
                    logits = temper * dots[:, at - start:at - start + LANES] + offset
                    hit = labcol[pl.ds(top, wide), :] == text_rows(at)
                    margin = jnp.where(hit, -logits, logits)
                    small = jnp.exp(-jnp.abs(logits))
                    base = 1.0 + small
                    inverse = 1.0 / base
                    log_part = jnp.log(base) + (small - (base - 1.0)) * inverse
                    loss = jnp.maximum(margin, 0.0) + log_part
                    loss_acc[0] += jnp.sum(loss.reshape(wide // 8, 8, LANES), axis=0)
                    slope = jnp.where(margin >= 0.0, 1.0, small) * inverse
                    slope = jnp.where(hit, -slope, slope).astype(jnp.bfloat16)
                    slopes[pl.ds(top, wide), at:at + LANES] = slope
                    slopes_t[at:at + LANES, pl.ds(top, wide)] = slope.T
            return carry

        lax.fori_loop(first, first + count, step, 0)

    def grad_images(first, count):
        gi[first * rows:(first + count) * rows, :] = jnp.dot(
            slopes[first * rows:(first + count) * rows, :], tbuf[...], preferred_element_type=jnp.float32)

    def grad_texts(first, count):
        gt[first * rows:(first + count) * rows, :] = jnp.dot(
            slopes_t[first * rows:(first + count) * rows, :], ibuf[...], preferred_element_type=jnp.float32)

    def packed(out, value):
        tops = jnp.max(jnp.abs(value).reshape(half // SCALE_ROWS, SCALE_ROWS, width), axis=0)
        top = tops[:, 0:LANES]
        for t in range(1, tiles):
            top = jnp.maximum(top, tops[:, t * LANES:(t + 1) * LANES])
        exponent = jnp.ceil(jnp.log2(jnp.maximum(top, 1e-30)))
        inverse = jnp.concatenate([jnp.exp2(TOP - exponent)] * (half // SCALE_ROWS), axis=0)
        out[tiles * half:tiles * half + SCALE_ROWS, :] = exponent.astype(jnp.int16)
        for t in range(tiles):
            scaled = jnp.round(value[:, t * LANES:(t + 1) * LANES] * inverse)
            out[t * half:(t + 1) * half, :] = scaled.astype(jnp.int32).astype(jnp.int16)

    def unpacked(message):
        exponent = message[tiles * half:tiles * half + SCALE_ROWS, :].astype(jnp.int32).astype(jnp.float32)
        scale = jnp.concatenate([jnp.exp2(exponent - TOP)] * (half // SCALE_ROWS), axis=0)
        return jnp.concatenate(
            [message[t * half:(t + 1) * half, :].astype(jnp.int32).astype(jnp.float32) * scale for t in range(tiles)],
            axis=1)

    def ring(kind, n, out, inbox, up, down, partial):
        halfway = n // 2

        def slot(hop, way, chunk):
            return (0 if way > 0 else 1), 2 * (hop - 1) + chunk

        def get(hop, way, chunk):
            box = inbox.at[slot(hop, way, chunk)]
            arrived((kind, hop, way, chunk), box, up)
            return unpacked(box)

        def put(hop, way, chunk):
            value = partial(way * (halfway + 1 - hop), chunk)
            fresh = hop == 1 or (hop == 2 and chunk == (B if way > 0 else A))
            if not fresh:
                value = value + get(hop - 1, way, chunk)
            at = slot(hop, way, chunk)
            packed(out.at[at], value)
            send((kind, hop, way, chunk), out.at[at], inbox.at[at], up if way > 0 else down)

        def last(chunk):
            return partial(0, chunk) + get(halfway, 1, chunk) + get(halfway, -1, chunk)

        return put, last

    z_put, z_last = ring("gz", NZ, zq_out, zq_in, z_up, z_down,
                         lambda rel, chunk: gi[image_at(rel, chunk):image_at(rel, chunk) + half, :])
    y_puts, y_lasts = [], []
    for p in (0, 1):
        put, last = ring(("gy", p), NY, yq_out.at[p], yq_in.at[p], y_up, y_down,
                         lambda rel, chunk, p=p: gt[text_at(rel, p, chunk):text_at(rel, p, chunk) + half, :])
        y_puts.append(put)
        y_lasts.append(last)

    loss_stages = [(z, z_others), (x, x_others), (core, [(1, twin)]), (y, y_others)]

    def loss_send(stage):
        at, others = loss_stages[stage]
        loss_in[stage, at] = loss_acc[stage]
        for d, peer in others:
            send(("loss", stage, d), loss_acc.at[stage], loss_in.at[stage, at], peer)

    def loss_get(stage):
        at, others = loss_stages[stage]
        for d, peer in others:
            arrived(("loss", stage, d), loss_in.at[stage, at], peer)
        total = loss_in[stage, 0]
        for k in range(1, len(others) + 1):
            total = total + loss_in[stage, k]
        loss_acc[stage + 1] = total

    def y_finish(p, chunk):
        tsum[p, part(chunk)] = y_lasts[p](chunk)
        packed(sq_out.at[p, chunk], tsum[p, part(chunk)])
        send(("gs", p, chunk), sq_out.at[p, chunk], sq_in.at[p, chunk], twin)

    def twin_get(p, chunk):
        arrived(("gs", p, chunk), sq_in.at[p, chunk], twin)

    def weight(who, home):
        return jnp.full((1, LANES), jnp.where(partner_ref[who] == home, 1.0, 0.0), jnp.float32)

    twin_group, across = x_lo * 2 + (1 - core), (1 - x_lo) * 2 + core
    here_weights = weight(group, group), weight(twin_group, group)
    there_weights = weight(group, across), weight(twin_group, across)

    def x_partial(what, chunk):
        p, (own_weight, twin_weight) = {
            OWN: (0, here_weights), NEAR: (0, there_weights), FAR: (1, there_weights), OPPOSITE: (1, here_weights)}[what]
        own, other = tsum[p, part(chunk)], unpacked(sq_in.at[p, chunk])
        return jnp.concatenate(
            [own[:, t * LANES:(t + 1) * LANES] * own_weight + other[:, t * LANES:(t + 1) * LANES] * twin_weight
             for t in range(tiles)], axis=1)

    def x_get(what, chunk):
        arrived(("gx", what, chunk), xq_in.at[what, chunk], near)
        return unpacked(xq_in.at[what, chunk])

    def x_put(what, chunk):
        value = x_partial(what, chunk)
        if what == (FAR if chunk == A else NEAR):
            value = value + x_get(OPPOSITE, chunk)
        packed(xq_out.at[what, chunk], value)
        peer = {NEAR: near, FAR: far, OPPOSITE: near if chunk == A else far}[what]
        send(("gx", what, chunk), xq_out.at[what, chunk], xq_in.at[what, chunk], peer)

    def write(out, chunk, value):
        out[0, part(chunk), :] = value

    x_pass(NEAR, 0)
    x_pass(FAR, 3)
    x_pass(NEAR, 1)
    x_pass(FAR, 4)
    choose(0, 0)
    y_send(1, 1, 0, 0)
    y_send(1, -1, 0, 0)
    x_pass(NEAR, 2)
    x_pass(FAR, 5)
    z_pass(1, 1, A)
    z_pass(1, -1, B)
    choose(0, 1)
    y_send(1, 1, 0, 1)
    y_send(1, -1, 0, 1)
    x_pass(NEAR, 3)
    x_pass(FAR, 0)
    choose(0, 2)
    y_send(1, 1, 0, 2)
    y_send(1, -1, 0, 2)
    x_pass(NEAR, 4)
    x_pass(FAR, 1)
    choose(0, 3)
    y_send(1, -1, 0, 3)
    y_send(1, 1, 0, 3)
    x_pass(NEAR, 5)
    x_pass(FAR, 2)
    z_pass(1, 1, B)
    z_pass(1, -1, A)
    y_pass(1, 1, 0, 0)
    y_pass(1, -1, 0, 0)
    choose(0, 4)
    y_send(1, -1, 0, 4)
    y_send(1, 1, 0, 4)
    x_pass(OPPOSITE, 3)
    x_pass(OPPOSITE, 0)
    y_pass(1, 1, 0, 1)
    y_pass(1, -1, 0, 1)
    choose(0, 5)
    y_send(1, -1, 0, 5)
    y_send(1, 1, 0, 5)
    x_pass(OPPOSITE, 4)
    x_pass(OPPOSITE, 1)
    y_pass(1, 1, 0, 2)
    y_pass(1, -1, 0, 2)
    choose(1, 3)
    y_send(1, -1, 1, 3)
    choose(1, 0)
    y_send(1, 1, 1, 0)
    x_pass(OPPOSITE, 5)
    x_pass(OPPOSITE, 2)
    z_pass(2, 1, A)
    z_pass(2, -1, B)
    y_pass(1, 1, 0, 3)
    y_pass(1, -1, 0, 3)
    choose(1, 4)
    y_send(1, -1, 1, 4)
    choose(1, 1)
    y_send(1, 1, 1, 1)
    y_pass(2, 1, 0, 0)
    y_pass(1, -1, 0, 4)
    choose(1, 5)
    y_send(1, -1, 1, 5)
    choose(1, 2)
    y_send(1, 1, 1, 2)
    y_pass(1, 1, 0, 4)
    y_pass(1, -1, 0, 5)
    y_send(1, 1, 1, 3)
    y_send(1, -1, 1, 0)
    y_send(1, 1, 1, 4)
    y_send(1, -1, 1, 1)
    y_send(1, 1, 1, 5)
    y_send(1, -1, 1, 2)
    z_pass(2, 1, B)
    z_pass(2, -1, A)
    label_columns((0, 1, 7, 2))
    y_pass(2, 1, 0, 1)
    y_pass(1, -1, 1, 3)
    y_pass(1, 1, 0, 5)
    y_pass(2, -1, 0, 3)
    y_pass(2, 1, 0, 2)
    y_pass(1, -1, 1, 4)
    z_pass(3, 1, A)
    z_pass(3, -1, B)
    y_pass(1, 1, 1, 0)
    y_pass(2, -1, 0, 4)
    y_pass(1, 1, 1, 1)
    y_pass(1, -1, 1, 5)
    y_pass(1, 1, 1, 2)
    y_pass(2, -1, 0, 5)
    z_pass(3, 1, B)
    z_pass(3, -1, A)
    label_columns((6, 3, 5))
    slope_tiles(0, 2, 0, 3 * LANES)
    y_pass(1, 1, 1, 3)
    y_pass(1, -1, 1, 0)
    y_pass(1, 1, 1, 4)
    y_pass(1, -1, 1, 1)
    y_pass(1, 1, 1, 5)
    y_pass(1, -1, 1, 2)
    slope_tiles(0, 2, 3 * LANES, 5 * LANES)
    z_pass(4, 1, A)
    z_pass(4, -1, B)
    label_columns((4,))
    slope_tiles(2, 1, 0, 3 * LANES)
    grad_texts(0, 4)
    y_puts[0](1, 1, A)
    y_puts[0](1, -1, B)
    slope_tiles(2, 1, 3 * LANES, 5 * LANES)
    y_pass(2, 1, 1, 0)
    y_pass(2, -1, 1, 3)
    y_pass(2, 1, 1, 1)
    y_pass(2, -1, 1, 4)
    y_pass(2, 1, 1, 2)
    y_pass(2, -1, 1, 5)
    slope_tiles(0, 3, 5 * LANES, 6 * LANES)

    loss_send(0)
    grad_texts(7, 1)
    y_puts[1](1, 1, A)
    y_puts[1](1, -1, B)
    grad_images(5, 3)
    z_put(1, 1, A)
    z_put(1, -1, B)
    z_put(2, 1, B)
    z_put(2, -1, A)
    grad_texts(4, 3)
    y_puts[1](2, 1, B)
    y_puts[1](2, -1, A)
    grad_images(0, 5)
    y_puts[1](2, 1, A)
    y_puts[1](2, -1, B)
    z_put(2, 1, A)
    z_put(2, -1, B)
    y_puts[0](2, 1, A)
    y_puts[0](2, -1, A)
    y_puts[0](2, -1, B)
    y_puts[0](2, 1, B)
    z_put(3, 1, B)
    z_put(3, -1, A)
    loss_get(0)
    loss_send(1)
    z_put(3, 1, A)
    z_put(3, -1, B)
    y_finish(1, A)
    y_finish(1, B)
    loss_get(1)
    loss_send(2)
    z_put(4, 1, B)
    z_put(4, -1, A)
    twin_get(1, A)
    x_put(OPPOSITE, A)
    twin_get(1, B)
    x_put(OPPOSITE, B)
    x_put(FAR, B)
    loss_get(2)
    loss_send(3)
    y_finish(0, A)
    z_put(4, 1, A)
    z_put(4, -1, B)
    twin_get(0, A)
    x_put(NEAR, A)
    y_finish(0, B)
    x_put(FAR, A)
    twin_get(0, B)
    x_put(NEAR, B)
    loss_get(3)
    loss_out[0] = jnp.sum(loss_acc[4]) / total_pairs
    for chunk in (A, B):
        write(img_out, chunk, z_last(chunk))
    for chunk in (A, B):
        write(txt_out, chunk, x_partial(OWN, chunk) + x_get(NEAR, chunk) + x_get(FAR, chunk))
    for copy in pending:
        copy.wait_send()


def shards(image_embeds, text_embeds, positives, partner, log_temp, bias):
    _, rows, width = image_embeds.shape
    half, tiles = rows // 2, width // LANES
    message = (tiles * half + SCALE_ROWS, LANES)
    n_i, n_t = NZ * rows, 2 * NY * rows
    cycle, groups = lax.axis_size("blk"), lax.axis_size("group")
    total_pairs = groups * rows * cycle * cycle
    vmem = pl.BlockSpec(memory_space=pltpu.VMEM)
    smem = pl.BlockSpec(memory_space=pltpu.SMEM)
    hbm = pl.BlockSpec(memory_space=pltpu.HBM)
    in_hbm = functools.partial(pltpu.with_memory_space_constraint, memory_space=pltpu.HBM)
    f32, bf16, i16, i32 = jnp.float32, jnp.bfloat16, jnp.int16, jnp.int32
    copies = 176
    images, texts, loss = pl.pallas_call(
        functools.partial(kernel, float(total_pairs)),
        out_shape=(jax.ShapeDtypeStruct((1, rows, width), f32), jax.ShapeDtypeStruct((1, rows, width), f32),
                   jax.ShapeDtypeStruct((1,), f32)),
        in_specs=[hbm] * 6,
        out_specs=(vmem, vmem, smem),
        scratch_shapes=[
            pltpu.SMEM(partner.shape, i32),
            pltpu.SMEM((1,), f32),
            pltpu.SMEM((1,), f32),
            pltpu.VMEM((1, rows), i32),
            pltpu.VMEM((n_i, width), bf16),
            pltpu.VMEM((n_t, width), bf16),
            pltpu.VMEM((2, NX, rows, width), bf16),
            pltpu.VMEM((NZ, 8, LANES), i32),
            pltpu.VMEM((n_i, LANES), i32),
            pltpu.VMEM((n_i, n_t), bf16),
            pltpu.VMEM((n_t, n_i), bf16),
            pltpu.VMEM((n_i, width), f32),
            pltpu.VMEM((n_t, width), f32),
            pltpu.VMEM((2, rows, width), f32),
            pltpu.VMEM((5, 8, LANES), f32),
            pltpu.VMEM((4, NZ, 8, LANES), f32),
            pltpu.VMEM((2, NZ, *message), i16),
            pltpu.VMEM((2, NZ, *message), i16),
            pltpu.VMEM((2, 2, NY, *message), i16),
            pltpu.VMEM((2, 2, NY, *message), i16),
            pltpu.VMEM((2, 2, *message), i16),
            pltpu.VMEM((2, 2, *message), i16),
            pltpu.VMEM((NX, 2, *message), i16),
            pltpu.VMEM((NX, 2, *message), i16),
            pltpu.SemaphoreType.DMA((copies,)),
            pltpu.SemaphoreType.DMA((copies,)),
            pltpu.SemaphoreType.DMA((6,)),
        ],
        compiler_params=pltpu.CompilerParams(
            collective_id=0, has_side_effects=True, vmem_limit_bytes=48 * 1024 * 1024),
    )(in_hbm(partner), log_temp, bias, in_hbm(image_embeds), in_hbm(text_embeds), in_hbm(positives))
    temper = jnp.exp(log_temp[0])
    return temper * images, temper * texts, loss


def solution(mesh):
    in_specs = (P("group", "blk", None), P("group", "blk", None), P("group", "blk"), P(), P(), P())
    out_specs = (P("group", "blk", None), P("group", "blk", None), P())
    return jax.shard_map(shards, mesh=mesh, in_specs=in_specs, out_specs=out_specs, check_vma=False)
```
